32 devices in a mesh: cols: 16 (over z, x, core), spec: 2 (over y).
Axes of the slice: x: 2, y: 2, z: 4, core: 2. Of those that a mesh axis runs over, the one named last changes fastest.
Arguments:
- air_state: float32 [8, 256, 64, 128], P(None, 'cols', 'spec'), may hold values from -13 to 13, as said below
- courant_x: float32 [128], replicated, may hold values from -0.45 to 0.45
- courant_y: float32 [128], replicated, may hold values from -0.45 to 0.45
- cos_zenith: float32 [256, 64], P('cols', 'spec'), may hold values from 0.15 to 1
- sun_index: int32 [16, 2, 96], P('cols', 'spec'), may hold values from 0 to 511, as said below
- sun_count: int32 [2, 16], replicated, may hold values from 1 to 96, 384 in all within a row
- in_weight: bfloat16 [7, 128], replicated, may hold values from -3 to 3
- in_bias: float32 [128], replicated, may hold values from -4 to 4
- mid_weight: bfloat16 [128, 128], replicated, may hold values from -0.099609375 to 0.099609375
- mid_bias: float32 [128], replicated, may hold values from -2 to 2
- out_weight: bfloat16 [128, 256, 128], P(None, 'spec'), may hold values from -0.5 to 0.5
- out_bias: float32 [256], P('spec'), may hold values from -3 to 3
- absorption: float32 [256], P('spec'), may hold values from 0.00390625 to 0.0625
- solar_flux: float32 [256], P('spec'), may hold values from 0.03 to 1
Outputs:
- new_state: float32 [8, 256, 64, 128], P(None, 'cols', 'spec')
- solar_heating: float32 [256, 64, 128], P('cols', 'spec')
The draws below stay inside these ranges and needn't reach their ends.
Inputs may be any that keep to these rules, and one draw needn't show every extreme that they name: For each tile (c, s) the entries sun_index[c, s, :] are distinct cell numbers m of that tile, naming the grid column (c * 16 + m // 32, s * 32 + m % 32); only the first sun_count[s, c] of them are sunlit, the others are unused. `sun_count`: entry [s, c] is the number of sunlit columns of tile (c, s); every row sums to exactly 384, and one entry of each row equals 96. `air_state`: the fields' values.
All inputs are finite; a program needn't handle non-finite values.
Results may differ from the reference program's by a relative error of at most 0.0023.
Values may be sent and summed in bfloat16 or wider, within the bound.
A program may use at most 64 MiB of HBM per device.

```python
import math
import jax
import jax.numpy as jnp
import numpy as np
from jax import lax

F = 8
NIN = 7
L = 128
HID = 128
G = 256
SECTIONS = 4
CX = 16
CY = 32
SUN_MAX = 96
SUN_MEAN = 24
GX = 16
GY = 2
NX = 256
NY = 64


def draw_sun_index(key, part):
    tile_keys = jax.random.split(key, GX * GY)

    def pick_cells(tile_key):
        return jax.random.permutation(tile_key, CX * CY)[:SUN_MAX]
    chosen = jax.vmap(pick_cells)(tile_keys)
    return chosen.reshape(GX, GY, SUN_MAX).astype(jnp.int32)


def draw_air_state(key, part):
    base_key, scale_key, offset_key = jax.random.split(jax.random.fold_in(key, 7), 3)
    base = jnp.clip(jax.random.normal(base_key, (F, NX, NY, L), jnp.float32), -4.0, 4.0)
    offset_span = 1.0
    column_scale = jnp.exp(jax.random.uniform(scale_key, (F, NX, NY, 1), jnp.float32, -1.5, 1.0))
    tile_offset = jax.random.uniform(offset_key, (F, GX, GY), jnp.float32, -offset_span, offset_span)
    spread_offset = jnp.repeat(jnp.repeat(tile_offset, CX, axis=1), CY, axis=2)[:, :, :, None]
    return (base * column_scale + spread_offset).astype(jnp.float32)


def shard_levels(stream_key, extent, cuts, smallest, top_value):
    def one(axis_at, shards_of):
        steps = jax.random.uniform(jax.random.fold_in(jax.random.fold_in(stream_key, 6), axis_at), (shards_of,), jnp.float32, smallest / len(cuts), top_value / len(cuts))
        return jnp.repeat(jnp.exp(steps), extent[axis_at] // shards_of).reshape((-1,) + (1,) * (len(extent) - axis_at - 1))

    level = one(*cuts[0])
    for cut in cuts[1:]:
        level = level * one(*cut)
    return level


def profile(amount, total, limit, skew):
    portions = [(1 << 20) // math.isqrt(grade ** skew) + 1 for grade in range(2, amount + 1)]
    surplus, given = total - limit - (amount - 1), [1] * (amount - 1)
    while surplus > 0:
        free = [i for i in range(amount - 1) if given[i] < limit]
        mass, budget = sum([portions[i] for i in free]), surplus
        for i in free:
            more = min(limit - given[i], max(1, budget * portions[i] // mass), surplus)
            given[i] = given[i] + more
            surplus = surplus - more
    return np.array([limit] + given)


def ragged(stream_key, number_of, total, limit, skew):
    if number_of == 2:
        one = jax.random.randint(stream_key, (), max(1, total - limit), min(limit, total - 1) + 1)
        return jnp.stack([one, total - one])
    tallies = jnp.asarray(profile(number_of, total, limit, skew), jnp.int32)
    twos = (number_of - 1) // 2
    source_of, sink = tallies[1:1 + 2 * twos:2], tallies[2:2 + 2 * twos:2]
    room = jnp.minimum(source_of - 1, limit - sink)
    passed = jax.random.randint(jax.random.fold_in(stream_key, 1), (twos,), 0, 1 << 20) % (room + 1)
    tallies = tallies.at[1:1 + 2 * twos:2].set(source_of - passed).at[2:2 + 2 * twos:2].set(sink + passed)
    return tallies[jax.random.permutation(jax.random.fold_in(stream_key, 2), number_of)]


def normal_values(rng, extent, scale, limit, pieces=(), kind=jnp.bfloat16):
    drawn = jax.random.normal(rng, extent, jnp.float32) * scale
    if len(pieces) > 0:
        drawn = shard_levels(rng, extent, pieces, -0.22, 0.18) * drawn
    return jnp.clip(drawn, min=-limit, max=limit).astype(kind)


def setup_inputs(seed: int = 0) -> dict:
    keys = jax.random.split(jax.random.key(seed), 15)
    return {
        "air_state": draw_air_state(jax.random.fold_in(keys[14], 71), 0),
        "courant_x": jnp.clip(jax.random.uniform(keys[1], (L,), jnp.float32, -0.45, 0.45), -0.45, 0.45),
        "courant_y": jnp.clip(jax.random.uniform(keys[2], (L,), jnp.float32, -0.45, 0.45), -0.45, 0.45),
        "cos_zenith": jnp.clip(0.15 + 0.85 * jax.random.uniform(keys[3], (NX, NY), jnp.float32) ** shard_levels(keys[3], (NX, NY), ((0, 16), (1, 2)), -0.2, 0.2), 0.15, 1.0),
        "sun_index": draw_sun_index(jax.random.fold_in(keys[14], 71), 0),
        "sun_count": jax.vmap(lambda own: ragged(own, GX, SUN_MEAN * GX, SUN_MAX, 2))(jax.random.split(keys[5], GY)).reshape((GY, GX)).astype(jnp.int32),
        "in_weight": jnp.clip(jax.random.uniform(keys[6], (NIN, HID), jnp.float32, -3.0, 3.0), -3.0, 3.0).astype(jnp.bfloat16),
        "in_bias": jnp.clip(jax.random.uniform(keys[7], (HID,), jnp.float32, -4.0, 4.0), -4.0, 4.0),
        "mid_weight": jnp.clip(jax.random.uniform(keys[8], (HID, HID), jnp.float32, -0.099609375, 0.099609375), -0.099609375, 0.099609375).astype(jnp.bfloat16),
        "mid_bias": jnp.clip(jax.random.uniform(keys[9], (HID,), jnp.float32, -2.0, 2.0), -2.0, 2.0),
        "out_weight": normal_values(keys[10], (L, G, HID), HID ** -0.5, 0.5, ((1, 2),)),
        "out_bias": normal_values(keys[11], (G,), 0.5, 3.0, ((0, 2),), jnp.float32),
        "absorption": jnp.clip(jnp.exp(math.log(0.0625) - 2.7725887 * jax.random.uniform(keys[12], (G,), jnp.float32) ** shard_levels(keys[12], (G,), ((0, 2),), -0.2, 0.2)), 0.00390625, 0.0625),
        "solar_flux": jnp.clip(jnp.exp(math.log(1.0) - 3.506558 * jax.random.uniform(keys[13], (G,), jnp.float32) ** shard_levels(keys[13], (G,), ((0, 2),), -0.2, 0.2)), 0.03, 1.0),
    }


DIFFUSION = 0.05
ALBEDO = 0.3
DIFFUSIVITY = 1.66


def advect(current, courant_x, courant_y):
    eastern = jnp.roll(current, -1, axis=1)
    western = jnp.roll(current, 1, axis=1)
    northern = jnp.roll(current, -1, axis=2)
    southern = jnp.roll(current, 1, axis=2)
    return (current - 0.5 * courant_x * (eastern - western)
            + (0.5 * courant_x * courant_x + DIFFUSION) * (eastern - 2.0 * current + western)
            - 0.5 * courant_y * (northern - southern)
            + (0.5 * courant_y * courant_y + DIFFUSION) * (northern - 2.0 * current + southern))


def radiate(features, slant_cos, in_weight, in_bias, mid_weight, mid_bias, out_weight, out_bias, absorption, solar_flux):
    features = lax.optimization_barrier(features)
    inputs = jnp.transpose(features, (2, 0, 1)).astype(jnp.float32)
    first_sum = jnp.einsum("lni,ih->lnh", inputs, in_weight.astype(jnp.float32))
    hidden_one = lax.optimization_barrier(jax.nn.silu(first_sum + in_bias).astype(jnp.bfloat16))
    second = jnp.einsum("lnh,hk->lnk", hidden_one.astype(jnp.float32), mid_weight.astype(jnp.float32))
    hidden_two = lax.optimization_barrier(jax.nn.silu(second + mid_bias).astype(jnp.bfloat16))
    logits = jnp.einsum("lgh,lnh->lgn", out_weight.astype(jnp.float32), hidden_two.astype(jnp.float32))
    depth_layer = absorption[:, None] * jax.nn.softplus(logits + out_bias[:, None])
    optical_depth = jnp.cumsum(depth_layer, axis=0)
    cosine = slant_cos.astype(jnp.float32)[None, None, :]
    column_total = optical_depth[-1:]
    source = solar_flux[None, :, None] * cosine
    down_top = source * jnp.exp(-(optical_depth - depth_layer) / cosine)
    down_bottom = source * jnp.exp(-optical_depth / cosine)
    up_base = ALBEDO * source * jnp.exp(-column_total / cosine)
    up_top = up_base * jnp.exp(-DIFFUSIVITY * (column_total - optical_depth + depth_layer))
    up_bottom = up_base * jnp.exp(-DIFFUSIVITY * (column_total - optical_depth))
    absorbed = down_top - down_bottom + up_bottom - up_top
    return jnp.transpose(jnp.sum(absorbed, axis=1))


def reference(air_state, courant_x, courant_y, cos_zenith, sun_index, sun_count, in_weight, in_bias, mid_weight, mid_bias, out_weight, out_bias, absorption, solar_flux):
    current = air_state
    for section_number in range(SECTIONS):
        current = advect(current, courant_x, courant_y)
    counts = jnp.transpose(sun_count).reshape(-1).astype(jnp.int32)
    count_ends = jnp.cumsum(counts).astype(jnp.int32)
    starts = count_ends - counts
    sunlit_total = SUN_MEAN * GX * GY
    rank_list = jnp.arange(sunlit_total, dtype=jnp.int32)
    tile_number = jnp.searchsorted(count_ends, rank_list, side="right").astype(jnp.int32)
    within = rank_list - starts[tile_number]
    tile_x = tile_number // GY
    tile_y = tile_number % GY
    cell_number = sun_index[tile_x, tile_y, within]
    cell_x = tile_x * CX + cell_number // CY
    cell_y = tile_y * CY + cell_number % CY
    features = jnp.transpose(air_state[:NIN][:, cell_x, cell_y, :], (1, 0, 2)).astype(jnp.bfloat16)
    slant_cos = cos_zenith[cell_x, cell_y].astype(jnp.bfloat16)
    block_rows = math.gcd(sunlit_total, 128)
    count_blocks = sunlit_total // block_rows
    shaped = (features.reshape(count_blocks, block_rows, NIN, L), slant_cos.reshape(count_blocks, block_rows))

    def one_block(block_pair):
        return radiate(block_pair[0], block_pair[1], in_weight, in_bias, mid_weight, mid_bias, out_weight, out_bias, absorption, solar_flux)

    heating = lax.map(one_block, shaped).reshape(sunlit_total, L)
    heat_grid = jnp.zeros((NX, NY, L), jnp.float32).at[cell_x, cell_y].add(heating)
    new_state = current.at[0].add(heat_grid)
    return (new_state, heat_grid)
```

```python
import functools

import jax
import jax.numpy as jnp
from jax import lax
from jax.experimental import pallas as pl
from jax.experimental.pallas import tpu as pltpu
from jax.sharding import PartitionSpec as P

SECTIONS = 4
DIFFUSION = 0.05
ALBEDO = 0.3
DIFFUSIVITY = 1.66
MESH = pl.DeviceIdType.MESH
F32 = jnp.float32
BF16 = jnp.bfloat16
VMEM_LIMIT = 56 * 1024 * 1024


def cell_column(ranks, counts, index_row, spec, col):
    row = lax.broadcasted_iota(jnp.int32, counts.shape, 0)
    column = lax.broadcasted_iota(jnp.int32, counts.shape, 1)
    values = jnp.where(row == spec, counts, 0).astype(F32)
    offset = jnp.sum(jnp.where(column < col, values, 0.0), axis=(0, 1), keepdims=True)
    own = jnp.sum(jnp.where(column == col, values, 0.0), axis=(0, 1), keepdims=True)
    place = lax.broadcasted_iota(jnp.int32, (1, index_row.shape[1]), 1).astype(F32)
    table = jnp.where(place < own, index_row.astype(F32) + 1.0, 0.0)
    found = jnp.where(ranks - offset == place, table, 0.0)
    return jnp.sum(found, axis=1, keepdims=True) - 1.0


def rank_column(parity, half, share):
    within = lax.broadcasted_iota(jnp.int32, (share, 1), 0)
    return jnp.concatenate(
        [((2 * k + parity) * share + within).astype(F32) for k in range(half)], axis=0
    )


def pack_kernel(share, half, width_y, halo, place_ref, air_ref, cos_ref, index_ref, count_ref,
                send_ref, xlow_ref, xhigh_ref, ylow_ref, yhigh_ref, picked):
    fields, cells, levels = air_ref.shape[0], air_ref.shape[1], air_ref.shape[2]
    width_x = cells // width_y
    inputs = fields - 1
    col, spec = place_ref[0], place_ref[1]
    for parity in range(2):
        cell = cell_column(
            rank_column(parity, half, share), count_ref[...], index_ref[0], spec, col
        )
        slots = cell.shape[0]
        lane = lax.broadcasted_iota(jnp.int32, (slots, cells), 1).astype(F32)
        choose = jnp.where(cell == lane, 1.0, 0.0).astype(BF16)
        for i in range(inputs):
            picked[i] = jnp.dot(
                choose, air_ref[i].astype(BF16), preferred_element_type=F32
            )
        cell_x = jnp.floor((cell + 0.5) * (1.0 / width_y))
        cell_y = cell - cell_x * width_y
        lane_x = lax.broadcasted_iota(jnp.int32, (slots, width_x), 1).astype(F32)
        lane_y = lax.broadcasted_iota(jnp.int32, (slots, width_y), 1).astype(F32)
        by_x = jnp.dot(
            jnp.where(cell_x == lane_x, 1.0, 0.0).astype(BF16),
            cos_ref[...].astype(BF16),
            preferred_element_type=F32,
        )
        slant = jnp.sum(jnp.where(cell_y == lane_y, by_x, 0.0), axis=1, keepdims=True)
        picked[inputs] = jnp.broadcast_to(slant, (slots, levels))
        for k in range(half):
            block = picked[:, k * share:(k + 1) * share, :]
            send_ref[parity, k] = block.reshape(fields * share, levels).astype(BF16)

    def cells_of(first, count):
        block = air_ref[:, pl.ds(first, count), :]
        return pltpu.einshape("fcl->cfl", block).reshape(count * fields, levels).astype(BF16)

    for x in range(halo):
        xlow_ref[x] = cells_of(x * width_y, width_y)
        xhigh_ref[x] = cells_of((width_x - halo + x) * width_y, width_y)
    for x in range(width_x):
        low = cells_of(x * width_y, 8)
        high = cells_of((x + 1) * width_y - 8, 8)
        ylow_ref[x] = low[:halo * fields]
        yhigh_ref[x] = high[(8 - halo) * fields:]


def exchange_kernel(cols, specs, halo, send_ref, xlow_ref, xhigh_ref, ylow_ref, yhigh_ref,
                    feat_ref, xl_ref, xh_ref, yl_ref, yh_ref,
                    pair_in, merged, group_in, send_sem, recv_sem, group_send, group_recv,
                    spec_send, spec_recv):
    col, spec = lax.axis_index("cols"), lax.axis_index("spec")
    half = cols // 2
    parity, k = lax.rem(col, 2), lax.div(col, 2)
    partner = col + 1 - 2 * parity
    east, west = lax.rem(col + 1, cols), lax.rem(col + cols - 1, cols)
    north, south = lax.rem(spec + 1, specs), lax.rem(spec + specs - 1, specs)
    barrier = pltpu.get_barrier_semaphore()
    peers = [(partner, spec), (east, spec), (west, spec)]
    peers += [(2 * lax.rem(k + d, half) + parity, spec) for d in range(1, half)]
    peers += [(col, lax.rem(spec + d, specs)) for d in range(1, specs)]
    for peer in peers:
        pl.semaphore_signal(barrier, inc=1, device_id=peer, device_id_type=MESH)
    pl.semaphore_wait(barrier, len(peers))

    def copy(src, dst, number, peer):
        return pltpu.make_async_remote_copy(
            src_ref=src, dst_ref=dst, send_sem=send_sem.at[number],
            recv_sem=recv_sem.at[number], device_id=peer, device_id_type=MESH,
        )

    width_x = ylow_ref.shape[0]
    rows = ylow_ref.shape[1]
    row_end = xlow_ref.shape[1]
    pair = copy(send_ref.at[1 - parity], pair_in, 0, (partner, spec))
    pair.start()
    sides = [
        copy(xlow_ref, xh_ref, 1, (west, spec)),
        copy(xhigh_ref, xl_ref, 2, (east, spec)),
        copy(ylow_ref, yh_ref.at[pl.ds(halo, width_x)], 3, (col, south)),
        copy(yhigh_ref, yl_ref.at[pl.ds(halo, width_x)], 4, (col, north)),
    ]
    pair.wait()
    merged[...] = send_ref[parity] + pair_in[...]
    groups = []
    for d in range(1, half):
        other = lax.rem(k + d, half)
        groups.append(pltpu.make_async_remote_copy(
            src_ref=merged.at[other], dst_ref=group_in.at[d - 1],
            send_sem=group_send.at[d - 1], recv_sem=group_recv.at[d - 1],
            device_id=(2 * other + parity, spec), device_id_type=MESH,
        ))
    for one in groups:
        one.start()
    for one in sides:
        one.start()
    for one in groups:
        one.wait()
    total = merged[k]
    for d in range(1, half):
        total = total + group_in[d - 1]
    feat_ref[spec] = total
    spreads = []
    for d in range(1, specs):
        spreads.append(pltpu.make_async_remote_copy(
            src_ref=feat_ref.at[spec], dst_ref=feat_ref.at[spec],
            send_sem=spec_send.at[d - 1], recv_sem=spec_recv.at[d - 1],
            device_id=(col, lax.rem(spec + d, specs)), device_id_type=MESH,
        ))
    for one in spreads:
        one.start()
    for one in sides:
        one.wait()
    corners = [
        copy(xl_ref.at[:, pl.ds(0, rows)], yh_ref.at[pl.ds(0, halo)], 5, (col, south)),
        copy(xh_ref.at[:, pl.ds(0, rows)], yh_ref.at[pl.ds(halo + width_x, halo)], 6, (col, south)),
        copy(xl_ref.at[:, pl.ds(row_end - rows, rows)], yl_ref.at[pl.ds(0, halo)], 7, (col, north)),
        copy(xh_ref.at[:, pl.ds(row_end - rows, rows)], yl_ref.at[pl.ds(halo + width_x, halo)], 8,
             (col, north)),
    ]
    for one in corners:
        one.start()
    for d in range(1, specs):
        spreads[d - 1].wait_send()
        source = lax.rem(spec + specs - d, specs)
        pltpu.make_async_remote_copy(
            src_ref=feat_ref.at[source], dst_ref=feat_ref.at[source],
            send_sem=spec_send.at[d - 1], recv_sem=spec_recv.at[d - 1],
            device_id=(col, lax.rem(spec + d, specs)), device_id_type=MESH,
        ).wait_recv()
    for one in corners:
        one.wait()


def silu(value):
    half = 0.5 * value
    return half + half * jnp.tanh(half)


def radiate_kernel(share, feat_ref, in_weight_ref, in_bias_ref, mid_weight_ref, mid_bias_ref,
                   out_weight_ref, out_bias_ref, absorption_ref, flux_ref, heat_ref,
                   feats, hidden, upward, down, heat):
    specs, rows, levels = feat_ref.shape
    fields = rows // share
    columns = specs * share
    block_levels = out_weight_ref.shape[0]
    step = pl.program_id(0)
    slant = jnp.concatenate(
        [feat_ref[s].astype(F32)[(fields - 1) * share:] for s in range(specs)], axis=0
    )[:, :1]

    @pl.when(step == 0)
    def _():
        for s in range(specs):
            feats[s * rows:(s + 1) * rows, :] = feat_ref[s].astype(F32)
        weight = jnp.concatenate(
            [in_weight_ref[...].astype(F32), jnp.zeros((1, in_weight_ref.shape[1]), F32)], axis=0
        ).astype(BF16)
        mid_weight = mid_weight_ref[...]
        in_bias, mid_bias = in_bias_ref[...], mid_bias_ref[...]

        @pl.loop(0, columns // 8)
        def _(group):
            s = group // (share // 8)
            first = s * rows + (group - s * (share // 8)) * 8
            ones = []
            for j in range(8):
                column = feats[pl.ds(first + j, fields, stride=share), :].astype(BF16)
                summed = lax.dot_general(
                    column, weight, (((0,), (0,)), ((), ())), preferred_element_type=F32
                )
                ones.append(silu(summed + in_bias).astype(BF16))
            second = jnp.dot(
                jnp.concatenate(ones, axis=0), mid_weight, preferred_element_type=F32
            )
            second = silu(second + mid_bias)
            for j in range(8):
                hidden[pl.ds(group * 8 + j, levels, stride=columns), :] = (
                    second[j * levels:(j + 1) * levels]
                )

        down[...] = flux_ref[...] * slant
        heat[...] = jnp.zeros_like(heat)

    absorption = absorption_ref[...]
    down_rate = -(absorption / slant)
    up_rate = -DIFFUSIVITY * absorption
    out_bias = out_bias_ref[...]
    lane = lax.broadcasted_iota(jnp.int32, (columns, levels), 1)

    @pl.loop(0, block_levels // 8)
    def _(part):
        now = down[...]
        total = heat[...]
        for j in range(8):
            local = part * 8 + j
            level = step * block_levels + local
            start = pl.multiple_of(level * columns, 8)
            two = hidden[pl.ds(start, columns), :].astype(BF16)
            logits = lax.dot_general(
                two, out_weight_ref[local], (((1,), (1,)), ((), ())), preferred_element_type=F32
            ) + out_bias
            small = jnp.exp(-jnp.abs(logits))
            soft = jnp.maximum(logits, 0.0) + jnp.where(
                small < 1e-3, small - 0.5 * small * small, jnp.log(1.0 + small)
            )
            below = now * jnp.exp(down_rate * soft)
            upward[level] = jnp.exp(up_rate * soft)
            gone = jnp.sum(now - below, axis=1, keepdims=True)
            total = jnp.where(lane == level, gone, total)
            now = below
        down[...] = now
        heat[...] = total

    @pl.when(step == pl.num_programs(0) - 1)
    def _():
        down[...] = ALBEDO * down[...]

        @pl.loop(0, levels // 8)
        def _(part):
            now = down[...]
            total = heat[...]
            for j in range(8):
                level = levels - 1 - (part * 8 + j)
                above = now * upward[level]
                gone = jnp.sum(now - above, axis=1, keepdims=True)
                total = jnp.where(lane == level, total + gone, total)
                now = above
            down[...] = now
            heat[...] = total

        heat_ref[...] = heat[...]


def gather_kernel(cols, specs, share, part_ref, heat_ref, spec_in, spec_send, spec_recv,
                  group_send, group_recv, pair_send, pair_recv):
    col, spec = lax.axis_index("cols"), lax.axis_index("spec")
    half = cols // 2
    parity, k = lax.rem(col, 2), lax.div(col, 2)
    partner = col + 1 - 2 * parity
    barrier = pltpu.get_barrier_semaphore()
    peers = [(partner, spec)]
    peers += [(2 * lax.rem(k + d, half) + parity, spec) for d in range(1, half)]
    peers += [(col, lax.rem(spec + d, specs)) for d in range(1, specs)]
    for peer in peers:
        pl.semaphore_signal(barrier, inc=1, device_id=peer, device_id_type=MESH)
    pl.semaphore_wait(barrier, len(peers))
    copies = []
    for d in range(1, specs):
        other = lax.rem(spec + d, specs)
        copies.append(pltpu.make_async_remote_copy(
            src_ref=part_ref.at[other], dst_ref=spec_in.at[d - 1],
            send_sem=spec_send.at[d - 1], recv_sem=spec_recv.at[d - 1],
            device_id=(col, other), device_id_type=MESH,
        ))
    for one in copies:
        one.start()
    for one in copies:
        one.wait()
    total = part_ref[spec]
    for d in range(1, specs):
        total = total + spec_in[d - 1]
    heat_ref[parity, k] = total
    groups = []
    for d in range(1, half):
        groups.append(pltpu.make_async_remote_copy(
            src_ref=heat_ref.at[parity, k], dst_ref=heat_ref.at[parity, k],
            send_sem=group_send.at[d - 1], recv_sem=group_recv.at[d - 1],
            device_id=(2 * lax.rem(k + d, half) + parity, spec), device_id_type=MESH,
        ))
    for one in groups:
        one.start()
    for d in range(1, half):
        groups[d - 1].wait_send()
        source = lax.rem(k + half - d, half)
        pltpu.make_async_remote_copy(
            src_ref=heat_ref.at[parity, source], dst_ref=heat_ref.at[parity, source],
            send_sem=group_send.at[d - 1], recv_sem=group_recv.at[d - 1],
            device_id=(2 * lax.rem(k + d, half) + parity, spec), device_id_type=MESH,
        ).wait_recv()
    pair = pltpu.make_async_remote_copy(
        src_ref=heat_ref.at[parity], dst_ref=heat_ref.at[parity],
        send_sem=pair_send, recv_sem=pair_recv,
        device_id=(partner, spec), device_id_type=MESH,
    )
    pair.start()
    pair.wait_send()
    pltpu.make_async_remote_copy(
        src_ref=heat_ref.at[1 - parity], dst_ref=heat_ref.at[1 - parity],
        send_sem=pair_send, recv_sem=pair_recv,
        device_id=(partner, spec), device_id_type=MESH,
    ).wait_recv()


def finish_kernel(share, halo, width_y, place_ref, air_ref, xl_ref, xh_ref, yl_ref, yh_ref,
                  courant_x_ref, courant_y_ref, index_ref, count_ref, heat_ref,
                  state_ref, grid_ref, first, second):
    fields, cells, levels = air_ref.shape
    width_x = cells // width_y
    col, spec = place_ref[0], place_ref[1]
    half = heat_ref.shape[1]
    wide_x, wide_y = width_x + 2 * halo, width_y + 2 * halo

    @pl.loop(0, width_x)
    def _(x):
        block = air_ref[:, pl.ds(pl.multiple_of(x * width_y, 8), width_y), :]
        first[x + halo, halo:halo + width_y] = pltpu.einshape("fcl->cfl", block)

    def unpacked(value, count):
        return value.astype(F32).reshape(count, fields, levels)

    for x in range(halo):
        first[x, halo:halo + width_y] = unpacked(xl_ref[x], width_y)
        first[halo + width_x + x, halo:halo + width_y] = unpacked(xh_ref[x], width_y)

    @pl.loop(0, wide_x)
    def _(x):
        first[x, 0:halo] = unpacked(yl_ref[x], halo)
        first[x, halo + width_y:wide_y] = unpacked(yh_ref[x], halo)

    rate_x, rate_y = courant_x_ref[...], courant_y_ref[...]
    spread_x = 0.5 * rate_x * rate_x + DIFFUSION
    spread_y = 0.5 * rate_y * rate_y + DIFFUSION

    def wide(row):
        return jnp.broadcast_to(row, (fields, levels))[None]

    keep = wide(1.0 - 2.0 * spread_x - 2.0 * spread_y)
    from_east, from_west = wide(spread_x - 0.5 * rate_x), wide(spread_x + 0.5 * rate_x)
    from_north, from_south = wide(spread_y - 0.5 * rate_y), wide(spread_y + 0.5 * rate_y)
    buffers = (first, second)
    for section in range(SECTIONS):
        source, target = buffers[section % 2], buffers[(section + 1) % 2]
        low, high = section + 1, wide_y - section - 1

        @pl.loop(section + 1, wide_x - section - 1)
        def _(x):
            target[x, low:high] = (
                keep * source[x, low:high]
                + from_east * source[x + 1, low:high]
                + from_west * source[x - 1, low:high]
                + from_north * source[x, low + 1:high + 1]
                + from_south * source[x, low - 1:high - 1]
            )

    done = buffers[SECTIONS % 2]
    grid = jnp.zeros((cells, levels), F32)
    for parity in range(2):
        cell = cell_column(
            rank_column(parity, half, share), count_ref[...], index_ref[0], spec, col
        )
        slots = cell.shape[0]
        lane = lax.broadcasted_iota(jnp.int32, (slots, cells), 1).astype(F32)
        choose = jnp.where(cell == lane, 1.0, 0.0).astype(BF16)
        rows = heat_ref[parity].reshape(slots, levels)
        upper = rows.astype(BF16)
        lower = (rows - upper.astype(F32)).astype(BF16)
        for piece in (upper, lower):
            grid = grid + lax.dot_general(
                choose, piece, (((0,), (0,)), ((), ())), preferred_element_type=F32
            )
    grid_ref[...] = grid

    @pl.loop(0, width_x)
    def _(x):
        block = done[x + halo, halo:halo + width_y]
        start = pl.multiple_of(x * width_y, 8)
        state_ref[:, pl.ds(start, width_y), :] = pltpu.einshape("cfl->fcl", block)
        state_ref[0, pl.ds(start, width_y), :] += grid_ref[pl.ds(start, width_y), :]


def on_device(
    air_state,
    courant_x,
    courant_y,
    cos_zenith,
    sun_index,
    sun_count,
    in_weight,
    in_bias,
    mid_weight,
    mid_bias,
    out_weight,
    out_bias,
    absorption,
    solar_flux,
):
    fields, width_x, width_y, levels = air_state.shape
    cells = width_x * width_y
    cols, specs = lax.axis_size("cols"), lax.axis_size("spec")
    half = cols // 2
    share = sun_index.shape[2] // 4
    halo = SECTIONS
    block_rows = fields * share
    air = air_state.reshape(fields, cells, levels)
    place = jnp.stack([lax.axis_index("cols"), lax.axis_index("spec")]).astype(jnp.int32)
    smem = pl.BlockSpec(memory_space=pltpu.SMEM)
    vmem = pl.BlockSpec(memory_space=pltpu.VMEM)
    dma = pltpu.SemaphoreType.DMA
    x_halo = jax.ShapeDtypeStruct((halo, width_y * fields, levels), BF16)
    params = pltpu.CompilerParams(vmem_limit_bytes=VMEM_LIMIT)

    packed = pl.pallas_call(
        functools.partial(pack_kernel, share, half, width_y, halo),
        out_shape=(
            jax.ShapeDtypeStruct((2, half, block_rows, levels), BF16),
            x_halo,
            x_halo,
            jax.ShapeDtypeStruct((width_x, halo * fields, levels), BF16),
            jax.ShapeDtypeStruct((width_x, halo * fields, levels), BF16),
        ),
        in_specs=[smem, vmem, vmem, vmem, vmem],
        out_specs=(vmem,) * 5,
        scratch_shapes=[pltpu.VMEM((fields, half * share, levels), F32)],
        compiler_params=params,
        name="pack",
    )(place, air, cos_zenith, sun_index, sun_count)

    y_halo = jax.ShapeDtypeStruct((width_x + 2 * halo, halo * fields, levels), BF16)
    features, x_low, x_high, y_low, y_high = pl.pallas_call(
        functools.partial(exchange_kernel, cols, specs, halo),
        out_shape=(
            jax.ShapeDtypeStruct((specs, block_rows, levels), BF16),
            x_halo,
            x_halo,
            y_halo,
            y_halo,
        ),
        in_specs=[vmem] * 5,
        out_specs=(vmem,) * 5,
        scratch_shapes=[
            pltpu.VMEM((half, block_rows, levels), BF16),
            pltpu.VMEM((half, block_rows, levels), BF16),
            pltpu.VMEM((half - 1, block_rows, levels), BF16),
            dma((9,)),
            dma((9,)),
            dma((half - 1,)),
            dma((half - 1,)),
            dma((specs - 1,)),
            dma((specs - 1,)),
        ],
        compiler_params=pltpu.CompilerParams(
            vmem_limit_bytes=VMEM_LIMIT, collective_id=0, has_side_effects=True
        ),
        name="exchange",
    )(*packed)

    columns = specs * share
    points = out_weight.shape[1]
    block_levels = 16

    def whole(shape):
        return pl.BlockSpec(shape, lambda i: (0,) * len(shape))

    operands = (
        features,
        in_weight,
        in_bias.reshape(1, -1),
        mid_weight,
        mid_bias.reshape(1, -1),
        out_weight,
        out_bias.reshape(1, -1),
        absorption.reshape(1, -1),
        solar_flux.reshape(1, -1),
    )
    specs_in = [whole(a.shape) for a in operands]
    specs_in[5] = pl.BlockSpec((block_levels,) + out_weight.shape[1:], lambda i: (i, 0, 0))
    partial_heat = pl.pallas_call(
        functools.partial(radiate_kernel, share),
        out_shape=jax.ShapeDtypeStruct((columns, levels), F32),
        grid=(levels // block_levels,),
        in_specs=specs_in,
        out_specs=whole((columns, levels)),
        scratch_shapes=[
            pltpu.VMEM((specs * block_rows, levels), F32),
            pltpu.VMEM((levels * columns, mid_weight.shape[1]), F32),
            pltpu.VMEM((levels, columns, points), F32),
            pltpu.VMEM((columns, points), F32),
            pltpu.VMEM((columns, levels), F32),
        ],
        compiler_params=params,
        name="radiate",
    )(*operands)

    heats = pl.pallas_call(
        functools.partial(gather_kernel, cols, specs, share),
        out_shape=jax.ShapeDtypeStruct((2, half, share, levels), F32),
        in_specs=[vmem],
        out_specs=vmem,
        scratch_shapes=[
            pltpu.VMEM((specs - 1, share, levels), F32),
            dma((specs - 1,)),
            dma((specs - 1,)),
            dma((half - 1,)),
            dma((half - 1,)),
            dma,
            dma,
        ],
        compiler_params=pltpu.CompilerParams(
            vmem_limit_bytes=VMEM_LIMIT, collective_id=1, has_side_effects=True
        ),
        name="gather",
    )(partial_heat.reshape(specs, share, levels))

    wide = (width_x + 2 * halo, width_y + 2 * halo, fields, levels)
    state, grid = pl.pallas_call(
        functools.partial(finish_kernel, share, halo, width_y),
        out_shape=(
            jax.ShapeDtypeStruct((fields, cells, levels), F32),
            jax.ShapeDtypeStruct((cells, levels), F32),
        ),
        in_specs=[smem] + [vmem] * 10,
        out_specs=(vmem, vmem),
        scratch_shapes=[pltpu.VMEM(wide, F32), pltpu.VMEM(wide, F32)],
        compiler_params=params,
        name="finish",
    )(place, air, x_low, x_high, y_low, y_high, courant_x.reshape(1, -1),
      courant_y.reshape(1, -1), sun_index, sun_count, heats)
    return (
        state.reshape(air_state.shape),
        grid.reshape(width_x, width_y, levels),
    )


def solution(mesh):
    placed = (
        P(None, "cols", "spec", None),
        P(),
        P(),
        P("cols", "spec"),
        P("cols", "spec", None),
        P(),
        P(),
        P(),
        P(),
        P(),
        P(None, "spec", None),
        P("spec"),
        P("spec"),
        P("spec"),
    )
    return jax.shard_map(
        on_device,
        mesh=mesh,
        in_specs=placed,
        out_specs=(P(None, "cols", "spec", None), P("cols", "spec", None)),
        check_vma=False,
    )
```

```python
import functools

import jax
import jax.numpy as jnp
from jax import lax
from jax.experimental import pallas as pl
from jax.experimental.pallas import tpu as pltpu
from jax.sharding import PartitionSpec as P

SECTIONS = 4
DIFFUSION = 0.05
ALBEDO = 0.3
DIFFUSIVITY = 1.66
MESH = pl.DeviceIdType.MESH
F32 = jnp.float32
BF16 = jnp.bfloat16
VMEM_LIMIT = 56 * 1024 * 1024


def cell_column(ranks, counts, index_row, spec, col):
    row = lax.broadcasted_iota(jnp.int32, counts.shape, 0)
    column = lax.broadcasted_iota(jnp.int32, counts.shape, 1)
    values = jnp.where(row == spec, counts, 0).astype(F32)
    offset = jnp.sum(jnp.where(column < col, values, 0.0), axis=(0, 1), keepdims=True)
    own = jnp.sum(jnp.where(column == col, values, 0.0), axis=(0, 1), keepdims=True)
    place = lax.broadcasted_iota(jnp.int32, (1, index_row.shape[1]), 1).astype(F32)
    table = jnp.where(place < own, index_row.astype(F32) + 1.0, 0.0)
    found = jnp.where(ranks - offset == place, table, 0.0)
    return jnp.sum(found, axis=1, keepdims=True) - 1.0


def rank_column(firsts, share):
    within = lax.broadcasted_iota(jnp.int32, (share, 1), 0)
    return jnp.concatenate([(first * share + within).astype(F32) for first in firsts], axis=0)


def silu(value):
    half = 0.5 * value
    return half + half * jnp.tanh(half)


def remote(src, dst, send, recv, peer):
    return pltpu.make_async_remote_copy(
        src_ref=src, dst_ref=dst, send_sem=send, recv_sem=recv, device_id=peer, device_id_type=MESH
    )


def main_kernel(cols, specs, share, halo, width_y,
                air_ref, cos_ref, index_ref, count_ref, courant_x_ref, courant_y_ref,
                in_weight_ref, in_bias_ref, mid_weight_ref, mid_bias_ref, out_weight_ref,
                out_bias_ref, absorption_ref, flux_ref,
                state_ref, heat_ref,
                send_ref, xlow_ref, xhigh_ref, ylow_ref, yhigh_ref, picked,
                feat_ref, xl_ref, xh_ref, yl_ref, yh_ref,
                pair_in, merged, next_in, narrowed, group_in,
                out_weight, feats, hidden, upward, part_ref, spec_in, first, second,
                weight_sem, send_sem, recv_sem, group_send, group_recv, spec_send, spec_recv,
                back_send, back_recv, heat_send, heat_recv):
    fields, cells, levels = air_ref.shape
    width_x = cells // width_y
    inputs = fields - 1
    wide_x, wide_y = width_x + 2 * halo, width_y + 2 * halo
    columns = specs * share
    block = fields * share
    col, spec = lax.axis_index("cols"), lax.axis_index("spec")
    half, quarter = cols // 2, cols // 4
    parity, k = lax.rem(col, 2), lax.div(col, 2)
    bit, kk = lax.rem(k, 2), lax.div(k, 2)
    partner = col + 1 - 2 * parity
    across = col + 2 - 4 * bit
    east, west = lax.rem(col + 1, cols), lax.rem(col + cols - 1, cols)
    north, south = lax.rem(spec + 1, specs), lax.rem(spec + specs - 1, specs)
    barrier = pltpu.get_barrier_semaphore()
    peers = [(partner, spec), (east, spec), (west, spec)]
    peers += [(2 * lax.rem(k + d, half) + parity, spec) for d in range(1, half)]
    peers += [(col, lax.rem(spec + d, specs)) for d in range(1, specs)]
    for peer in peers:
        pl.semaphore_signal(barrier, inc=1, device_id=peer, device_id_type=MESH)
    fetch = pltpu.make_async_copy(out_weight_ref, out_weight, weight_sem)
    fetch.start()

    def copy(src, dst, number, peer):
        return remote(src, dst, send_sem.at[number], recv_sem.at[number], peer)

    counts, index_row = count_ref[...], index_ref[0]

    def pack(which):
        ranks = rank_column(
            [4 * c + 2 * b + which for b in range(2) for c in range(quarter)], share
        )
        cell = cell_column(ranks, counts, index_row, spec, col)
        slots = cell.shape[0]
        lane = lax.broadcasted_iota(jnp.int32, (slots, cells), 1).astype(F32)
        choose = jnp.where(cell == lane, 1.0, 0.0).astype(BF16)
        for i in range(inputs):
            picked[i] = jnp.dot(choose, air_ref[i].astype(BF16), preferred_element_type=F32)
        cell_x = jnp.floor((cell + 0.5) * (1.0 / width_y))
        cell_y = cell - cell_x * width_y
        lane_x = lax.broadcasted_iota(jnp.int32, (slots, width_x), 1).astype(F32)
        lane_y = lax.broadcasted_iota(jnp.int32, (slots, width_y), 1).astype(F32)
        by_x = jnp.dot(
            jnp.where(cell_x == lane_x, 1.0, 0.0).astype(BF16),
            cos_ref[...].astype(BF16),
            preferred_element_type=F32,
        )
        slant = jnp.sum(jnp.where(cell_y == lane_y, by_x, 0.0), axis=1, keepdims=True)
        picked[inputs] = jnp.broadcast_to(slant, (slots, levels))
        blocks = []
        for at in range(half):
            piece = picked[:, at * share:(at + 1) * share, :]
            blocks.append(piece.reshape(block, levels).astype(BF16)[None])
        return jnp.concatenate(blocks, axis=0).reshape(2, quarter, block, levels)

    send_ref[...] = pack(1 - parity)
    pl.semaphore_wait(barrier, len(peers))
    pair = copy(send_ref, pair_in, 0, (partner, spec))
    pair.start()
    merged[...] = pack(parity)
    pair.wait()
    merged[...] = merged[...] + pair_in[...]
    over = copy(merged.at[1 - bit], next_in, 9, (across, spec))
    over.start()

    def cells_of(start, count):
        piece = air_ref[:, pl.ds(start, count), :]
        return pltpu.einshape("fcl->cfl", piece).reshape(count * fields, levels).astype(BF16)

    for x in range(halo):
        xlow_ref[x] = cells_of(x * width_y, width_y)
        xhigh_ref[x] = cells_of((width_x - halo + x) * width_y, width_y)
    over.wait()
    narrowed[...] = merged[bit] + next_in[...]
    groups = []
    for d in range(1, quarter):
        other = lax.rem(kk + d, quarter)
        groups.append(remote(
            narrowed.at[other], group_in.at[d - 1], group_send.at[d - 1], group_recv.at[d - 1],
            (4 * other + 2 * bit + parity, spec),
        ))
    for one in groups:
        one.start()

    @pl.loop(0, width_x)
    def _(x):
        low = cells_of(pl.multiple_of(x * width_y, 8), 8)
        high = cells_of(pl.multiple_of(x * width_y + width_y - 8, 8), 8)
        ylow_ref[x] = low[:halo * fields]
        yhigh_ref[x] = high[(8 - halo) * fields:]

    for one in groups:
        one.wait()
    total = narrowed[kk]
    for d in range(1, quarter):
        total = total + group_in[d - 1]
    feat_ref[spec] = total
    spreads = []
    for d in range(1, specs):
        spreads.append(remote(
            feat_ref.at[spec], feat_ref.at[spec], spec_send.at[d - 1], spec_recv.at[d - 1],
            (col, lax.rem(spec + d, specs)),
        ))
    for one in spreads:
        one.start()
    rows = ylow_ref.shape[1]
    row_end = xlow_ref.shape[1]
    sides = [
        copy(xlow_ref, xh_ref, 1, (west, spec)),
        copy(xhigh_ref, xl_ref, 2, (east, spec)),
        copy(ylow_ref, yh_ref.at[pl.ds(halo, width_x)], 3, (col, south)),
        copy(yhigh_ref, yl_ref.at[pl.ds(halo, width_x)], 4, (col, north)),
    ]
    for one in sides:
        one.start()

    @pl.loop(0, width_x)
    def _(x):
        piece = air_ref[:, pl.ds(pl.multiple_of(x * width_y, 8), width_y), :]
        first[x + halo, halo:halo + width_y] = pltpu.einshape("fcl->cfl", piece)

    for d in range(1, specs):
        spreads[d - 1].wait_send()
        source = lax.rem(spec + specs - d, specs)
        remote(
            feat_ref.at[source], feat_ref.at[source], spec_send.at[d - 1], spec_recv.at[d - 1],
            (col, lax.rem(spec + d, specs)),
        ).wait_recv()

    for s in range(specs):
        feats[s * block:(s + 1) * block, :] = feat_ref[s].astype(F32)
    slant = jnp.concatenate(
        [feats[s * block + inputs * share:(s + 1) * block, :] for s in range(specs)], axis=0
    )[:, :1]
    weight = jnp.concatenate(
        [in_weight_ref[...].astype(F32), jnp.zeros((1, in_weight_ref.shape[1]), F32)], axis=0
    ).astype(BF16)
    mid_weight = mid_weight_ref[...]
    in_bias, mid_bias = in_bias_ref[...], mid_bias_ref[...]

    for s in range(specs):
        @pl.loop(0, share // 8)
        def _(group):
            ones = []
            for j in range(8):
                column = feats[pl.ds(s * block + group * 8 + j, fields, stride=share), :]
                summed = lax.dot_general(
                    column.astype(BF16), weight, (((0,), (0,)), ((), ())),
                    preferred_element_type=F32,
                )
                ones.append(silu(summed + in_bias).astype(BF16))
            middle = jnp.dot(
                jnp.concatenate(ones, axis=0), mid_weight, preferred_element_type=F32
            )
            middle = silu(middle + mid_bias)
            for j in range(8):
                start = s * share + group * 8 + j
                hidden[pl.ds(start, levels, stride=columns), :] = (
                    middle[j * levels:(j + 1) * levels]
                )

    for one in sides:
        one.wait()
    corners = [
        copy(xl_ref.at[:, pl.ds(0, rows)], yh_ref.at[pl.ds(0, halo)], 5, (col, south)),
        copy(xh_ref.at[:, pl.ds(0, rows)], yh_ref.at[pl.ds(halo + width_x, halo)], 6, (col, south)),
        copy(xl_ref.at[:, pl.ds(row_end - rows, rows)], yl_ref.at[pl.ds(0, halo)], 7, (col, north)),
        copy(xh_ref.at[:, pl.ds(row_end - rows, rows)], yl_ref.at[pl.ds(halo + width_x, halo)], 8,
             (col, north)),
    ]
    for one in corners:
        one.start()
    fetch.wait()

    absorption = absorption_ref[...]
    down_rate = -(absorption / slant)
    up_rate = -DIFFUSIVITY * absorption
    out_bias = out_bias_ref[...]
    lane = lax.broadcasted_iota(jnp.int32, (columns, levels), 1)
    unroll = 16

    def downward(part, carry):
        now, kept = carry
        for j in range(unroll):
            level = part * unroll + j
            start = pl.multiple_of(level * columns, 8)
            two = hidden[pl.ds(start, columns), :].astype(BF16)
            logits = lax.dot_general(
                two, out_weight[level], (((1,), (1,)), ((), ())), preferred_element_type=F32
            ) + out_bias
            small = jnp.exp(-jnp.abs(logits))
            soft = jnp.maximum(logits, 0.0) + jnp.where(
                small < 1e-3, small - 0.5 * small * small, jnp.log(1.0 + small)
            )
            below = now * jnp.exp(down_rate * soft)
            upward[level] = jnp.exp(up_rate * soft)
            gone = jnp.sum(now - below, axis=1, keepdims=True)
            kept = jnp.where(lane == level, gone, kept)
            now = below
        return now, kept

    def upwards(part, carry):
        now, kept = carry
        for j in range(unroll):
            level = levels - 1 - (part * unroll + j)
            above = now * upward[level]
            gone = jnp.sum(now - above, axis=1, keepdims=True)
            kept = jnp.where(lane == level, kept + gone, kept)
            now = above
        return now, kept

    now, kept = lax.fori_loop(
        0, levels // unroll, downward,
        (flux_ref[...] * slant, jnp.zeros((columns, levels), F32)),
    )
    _, kept = lax.fori_loop(0, levels // unroll, upwards, (ALBEDO * now, kept))
    part_ref[...] = kept.reshape(specs, share, levels)

    backs = []
    for d in range(1, specs):
        other = lax.rem(spec + d, specs)
        backs.append(remote(
            part_ref.at[other], spec_in.at[d - 1], back_send.at[d - 1], back_recv.at[d - 1],
            (col, other),
        ))
    for one in backs:
        one.start()

    for one in corners:
        one.wait()

    def unpacked(value, count):
        return value.astype(F32).reshape(count, fields, levels)

    for x in range(halo):
        first[x, halo:halo + width_y] = unpacked(xl_ref[x], width_y)
        first[halo + width_x + x, halo:halo + width_y] = unpacked(xh_ref[x], width_y)

    @pl.loop(0, wide_x)
    def _(x):
        first[x, 0:halo] = unpacked(yl_ref[x], halo)
        first[x, halo + width_y:wide_y] = unpacked(yh_ref[x], halo)

    rate_x, rate_y = courant_x_ref[...], courant_y_ref[...]
    spread_x = 0.5 * rate_x * rate_x + DIFFUSION
    spread_y = 0.5 * rate_y * rate_y + DIFFUSION

    def wide(row):
        return jnp.broadcast_to(row, (fields, levels))[None]

    keep = wide(1.0 - 2.0 * spread_x - 2.0 * spread_y)
    from_east, from_west = wide(spread_x - 0.5 * rate_x), wide(spread_x + 0.5 * rate_x)
    from_north, from_south = wide(spread_y - 0.5 * rate_y), wide(spread_y + 0.5 * rate_y)
    buffers = (first, second)

    def advance(section):
        source, target = buffers[section % 2], buffers[(section + 1) % 2]
        low, high = section + 1, wide_y - section - 1
        last = section == SECTIONS - 1

        @pl.loop(section + 1, wide_x - section - 1)
        def _(x):
            value = (
                keep * source[x, low:high]
                + from_east * source[x + 1, low:high]
                + from_west * source[x - 1, low:high]
                + from_north * source[x, low + 1:high + 1]
                + from_south * source[x, low - 1:high - 1]
            )
            if last:
                state_ref[x - halo] = value
            else:
                target[x, low:high] = value

    for one in backs:
        one.wait()
    total = part_ref[spec]
    for d in range(1, specs):
        total = total + spec_in[d - 1]
    heat_ref[parity, k] = total
    gathers = []
    for d in range(1, half):
        gathers.append(remote(
            heat_ref.at[parity, k], heat_ref.at[parity, k], heat_send.at[d], heat_recv.at[d],
            (2 * lax.rem(k + d, half) + parity, spec),
        ))
    for one in gathers:
        one.start()
    for section in range(SECTIONS - 1):
        advance(section)
    for d in range(1, half):
        gathers[d - 1].wait_send()
        source = lax.rem(k + half - d, half)
        remote(
            heat_ref.at[parity, source], heat_ref.at[parity, source],
            heat_send.at[d], heat_recv.at[d],
            (2 * lax.rem(k + d, half) + parity, spec),
        ).wait_recv()
    last = remote(
        heat_ref.at[parity], heat_ref.at[parity], heat_send.at[0], heat_recv.at[0],
        (partner, spec),
    )
    last.start()
    advance(SECTIONS - 1)
    last.wait_send()
    remote(
        heat_ref.at[1 - parity], heat_ref.at[1 - parity], heat_send.at[0], heat_recv.at[0],
        (partner, spec),
    ).wait_recv()


def finish_kernel(share, width_y, place_ref, state_in_ref, index_ref, count_ref, heat_ref,
                  state_ref, grid_ref):
    cells, levels = grid_ref.shape
    width_x = cells // width_y
    col, spec = place_ref[0], place_ref[1]
    half = heat_ref.shape[1]
    grid = jnp.zeros((cells, levels), F32)
    for parity in range(2):
        ranks = rank_column([2 * k + parity for k in range(half)], share)
        cell = cell_column(ranks, count_ref[...], index_ref[0], spec, col)
        slots = cell.shape[0]
        lane = lax.broadcasted_iota(jnp.int32, (slots, cells), 1).astype(F32)
        choose = jnp.where(cell == lane, 1.0, 0.0).astype(BF16)
        rows = heat_ref[parity].reshape(slots, levels)
        upper = rows.astype(BF16)
        lower = (rows - upper.astype(F32)).astype(BF16)
        for piece in (upper, lower):
            grid = grid + lax.dot_general(
                choose, piece, (((0,), (0,)), ((), ())), preferred_element_type=F32
            )
    grid_ref[...] = grid

    @pl.loop(0, width_x)
    def _(x):
        start = pl.multiple_of(x * width_y, 8)
        state_ref[:, pl.ds(start, width_y), :] = pltpu.einshape("cfl->fcl", state_in_ref[x])
        state_ref[0, pl.ds(start, width_y), :] += grid_ref[pl.ds(start, width_y), :]


def on_device(
    air_state,
    courant_x,
    courant_y,
    cos_zenith,
    sun_index,
    sun_count,
    in_weight,
    in_bias,
    mid_weight,
    mid_bias,
    out_weight,
    out_bias,
    absorption,
    solar_flux,
):
    fields, width_x, width_y, levels = air_state.shape
    cells = width_x * width_y
    cols, specs = lax.axis_size("cols"), lax.axis_size("spec")
    half, quarter = cols // 2, cols // 4
    share = sun_index.shape[2] // 4
    halo = SECTIONS
    block = fields * share
    columns = specs * share
    points, hidden_size = out_weight.shape[1], out_weight.shape[2]
    air = air_state.reshape(fields, cells, levels)
    place = jnp.stack([lax.axis_index("cols"), lax.axis_index("spec")]).astype(jnp.int32)
    smem = pl.BlockSpec(memory_space=pltpu.SMEM)
    vmem = pl.BlockSpec(memory_space=pltpu.VMEM)
    dma = pltpu.SemaphoreType.DMA
    x_halo = pltpu.VMEM((halo, width_y * fields, levels), BF16)
    y_edge = pltpu.VMEM((width_x, halo * fields, levels), BF16)
    y_halo = pltpu.VMEM((width_x + 2 * halo, halo * fields, levels), BF16)
    wide = pltpu.VMEM((width_x + 2 * halo, width_y + 2 * halo, fields, levels), F32)

    state, heats = pl.pallas_call(
        functools.partial(main_kernel, cols, specs, share, halo, width_y),
        out_shape=(
            jax.ShapeDtypeStruct((width_x, width_y, fields, levels), F32),
            jax.ShapeDtypeStruct((2, half, share, levels), F32),
        ),
        in_specs=[vmem] * 10 + [pl.BlockSpec(memory_space=pl.ANY)] + [vmem] * 3,
        out_specs=(vmem, vmem),
        scratch_shapes=[
            pltpu.VMEM((2, quarter, block, levels), BF16),
            x_halo,
            x_halo,
            y_edge,
            y_edge,
            pltpu.VMEM((fields, half * share, levels), F32),
            pltpu.VMEM((specs, block, levels), BF16),
            x_halo,
            x_halo,
            y_halo,
            y_halo,
            pltpu.VMEM((2, quarter, block, levels), BF16),
            pltpu.VMEM((2, quarter, block, levels), BF16),
            pltpu.VMEM((quarter, block, levels), BF16),
            pltpu.VMEM((quarter, block, levels), BF16),
            pltpu.VMEM((quarter - 1, block, levels), BF16),
            pltpu.VMEM(out_weight.shape, BF16),
            pltpu.VMEM((specs * block, levels), F32),
            pltpu.VMEM((levels * columns, hidden_size), F32),
            pltpu.VMEM((levels, columns, points), F32),
            pltpu.VMEM((specs, share, levels), F32),
            pltpu.VMEM((specs - 1, share, levels), F32),
            wide,
            wide,
            dma,
            dma((10,)),
            dma((10,)),
            dma((quarter - 1,)),
            dma((quarter - 1,)),
            dma((specs - 1,)),
            dma((specs - 1,)),
            dma((specs - 1,)),
            dma((specs - 1,)),
            dma((half,)),
            dma((half,)),
        ],
        compiler_params=pltpu.CompilerParams(
            vmem_limit_bytes=VMEM_LIMIT, collective_id=0, has_side_effects=True
        ),
        name="main",
    )(air, cos_zenith, sun_index, sun_count, courant_x.reshape(1, -1), courant_y.reshape(1, -1),
      in_weight, in_bias.reshape(1, -1), mid_weight, mid_bias.reshape(1, -1), out_weight,
      out_bias.reshape(1, -1), absorption.reshape(1, -1), solar_flux.reshape(1, -1))

    state, grid = pl.pallas_call(
        functools.partial(finish_kernel, share, width_y),
        out_shape=(
            jax.ShapeDtypeStruct((fields, cells, levels), F32),
            jax.ShapeDtypeStruct((cells, levels), F32),
        ),
        in_specs=[smem] + [vmem] * 4,
        out_specs=(vmem, vmem),
        compiler_params=pltpu.CompilerParams(vmem_limit_bytes=VMEM_LIMIT),
        name="finish",
    )(place, state, sun_index, sun_count, heats)
    return (
        state.reshape(air_state.shape),
        grid.reshape(width_x, width_y, levels),
    )


def solution(mesh):
    placed = (
        P(None, "cols", "spec", None),
        P(),
        P(),
        P("cols", "spec"),
        P("cols", "spec", None),
        P(),
        P(),
        P(),
        P(),
        P(),
        P(None, "spec", None),
        P("spec"),
        P("spec"),
        P("spec"),
    )
    return jax.shard_map(
        on_device,
        mesh=mesh,
        in_specs=placed,
        out_specs=(P(None, "cols", "spec", None), P("cols", "spec", None)),
        check_vma=False,
    )
```

```python
import functools

import jax
import jax.numpy as jnp
from jax import lax
from jax.experimental import pallas as pl
from jax.experimental.pallas import tpu as pltpu
from jax.sharding import PartitionSpec as P

SECTIONS = 4
CHUNKS = 2
LOG2_E = 1.4426950408889634
DIFFUSION = 0.05
ALBEDO = 0.3
DIFFUSIVITY = 1.66
MESH = pl.DeviceIdType.MESH
F32 = jnp.float32
BF16 = jnp.bfloat16
VMEM_LIMIT = 56 * 1024 * 1024


def cell_column(ranks, counts, index_row, spec, col):
    row = lax.broadcasted_iota(jnp.int32, counts.shape, 0)
    column = lax.broadcasted_iota(jnp.int32, counts.shape, 1)
    values = jnp.where(row == spec, counts, 0).astype(F32)
    offset = jnp.sum(jnp.where(column < col, values, 0.0), axis=(0, 1), keepdims=True)
    own = jnp.sum(jnp.where(column == col, values, 0.0), axis=(0, 1), keepdims=True)
    place = lax.broadcasted_iota(jnp.int32, (1, index_row.shape[1]), 1).astype(F32)
    table = jnp.where(place < own, index_row.astype(F32) + 1.0, 0.0)
    found = jnp.where(ranks - offset == place, table, 0.0)
    return jnp.sum(found, axis=1, keepdims=True) - 1.0


def rank_column(firsts, share):
    within = lax.broadcasted_iota(jnp.int32, (share, 1), 0)
    return jnp.concatenate([(first * share + within).astype(F32) for first in firsts], axis=0)


def silu(value):
    half = 0.5 * value
    return half + half * jnp.tanh(half)


def remote(src, dst, send, recv, peer):
    return pltpu.make_async_remote_copy(
        src_ref=src, dst_ref=dst, send_sem=send, recv_sem=recv, device_id=peer, device_id_type=MESH
    )


def main_kernel(cols, specs, share, halo, width_y,
                air_ref, cos_ref, index_ref, count_ref, courant_x_ref, courant_y_ref,
                in_weight_ref, in_bias_ref, mid_weight_ref, mid_bias_ref, out_weight_ref,
                out_bias_ref, absorption_ref, flux_ref,
                state_ref, heat_ref,
                send_ref, xlow_ref, xhigh_ref, ylow_ref, yhigh_ref, picked,
                feat_ref, xl_ref, xh_ref, yl_ref, yh_ref,
                pair_in, merged, next_in, narrowed, group_in,
                out_weight, feats, hidden, upward, part_ref, spec_in, first, second,
                weight_sem, send_sem, recv_sem, group_send, group_recv, spec_send, spec_recv,
                back_send, back_recv, heat_send, heat_recv):
    fields, cells, levels = air_ref.shape
    width_x = cells // width_y
    inputs = fields - 1
    wide_x, wide_y = width_x + 2 * halo, width_y + 2 * halo
    columns = specs * share
    block = fields * share
    group_fields = fields // CHUNKS
    piece_rows = group_fields * share
    col, spec = lax.axis_index("cols"), lax.axis_index("spec")
    half, quarter = cols // 2, cols // 4
    parity, k = lax.rem(col, 2), lax.div(col, 2)
    bit, kk = lax.rem(k, 2), lax.div(k, 2)
    partner = col + 1 - 2 * parity
    across = col + 2 - 4 * bit
    east, west = lax.rem(col + 1, cols), lax.rem(col + cols - 1, cols)
    north, south = lax.rem(spec + 1, specs), lax.rem(spec + specs - 1, specs)
    barrier = pltpu.get_barrier_semaphore()
    peers = [(partner, spec), (east, spec), (west, spec)]
    peers += [(2 * lax.rem(k + d, half) + parity, spec) for d in range(1, half)]
    peers += [(col, lax.rem(spec + d, specs)) for d in range(1, specs)]
    for peer in peers:
        pl.semaphore_signal(barrier, inc=1, device_id=peer, device_id_type=MESH)
    fetch = pltpu.make_async_copy(out_weight_ref, out_weight, weight_sem)
    fetch.start()

    def copy(src, dst, number, peer):
        return remote(src, dst, send_sem.at[number], recv_sem.at[number], peer)

    counts, index_row = count_ref[...], index_ref[0]

    def choice(which):
        ranks = rank_column(
            [4 * c + 2 * b + which for b in range(2) for c in range(quarter)], share
        )
        cell = cell_column(ranks, counts, index_row, spec, col)
        slots = cell.shape[0]
        lane = lax.broadcasted_iota(jnp.int32, (slots, cells), 1).astype(F32)
        choose = jnp.where(cell == lane, 1.0, 0.0).astype(BF16)
        return cell, choose

    def pack(chosen, chunk):
        cell, choose = chosen
        slots = cell.shape[0]
        for at in range(group_fields):
            i = chunk * group_fields + at
            if i < inputs:
                picked[at] = jnp.dot(
                    choose, air_ref[i].astype(BF16), preferred_element_type=F32
                )
                continue
            cell_x = jnp.floor((cell + 0.5) * (1.0 / width_y))
            cell_y = cell - cell_x * width_y
            lane_x = lax.broadcasted_iota(jnp.int32, (slots, width_x), 1).astype(F32)
            lane_y = lax.broadcasted_iota(jnp.int32, (slots, width_y), 1).astype(F32)
            by_x = jnp.dot(
                jnp.where(cell_x == lane_x, 1.0, 0.0).astype(BF16),
                cos_ref[...].astype(BF16),
                preferred_element_type=F32,
            )
            slant = jnp.sum(jnp.where(cell_y == lane_y, by_x, 0.0), axis=1, keepdims=True)
            picked[at] = jnp.broadcast_to(slant, (slots, levels))
        blocks = []
        for at in range(half):
            piece = picked[:, at * share:(at + 1) * share, :]
            blocks.append(piece.reshape(piece_rows, levels).astype(BF16)[None])
        return jnp.concatenate(blocks, axis=0).reshape(2, quarter, piece_rows, levels)

    chosen = choice(1 - parity)
    pairs = [
        copy(send_ref.at[c], pair_in.at[c], 10 + c, (partner, spec)) for c in range(CHUNKS)
    ]
    overs = [
        copy(merged.at[c, 1 - bit], next_in.at[c], 10 + CHUNKS + c, (across, spec))
        for c in range(CHUNKS)
    ]
    for c in range(CHUNKS):
        send_ref[c] = pack(chosen, c)
        if c == 0:
            pl.semaphore_wait(barrier, len(peers))
        pairs[c].start()
    chosen = choice(parity)
    for c in range(CHUNKS):
        merged[c] = pack(chosen, c)
        pairs[c].wait()
        merged[c] = merged[c] + pair_in[c]
        overs[c].start()

    def cells_of(start, count):
        piece = air_ref[:, pl.ds(start, count), :]
        return pltpu.einshape("fcl->cfl", piece).reshape(count * fields, levels).astype(BF16)

    for x in range(halo):
        xlow_ref[x] = cells_of(x * width_y, width_y)
        xhigh_ref[x] = cells_of((width_x - halo + x) * width_y, width_y)
    groups = []
    for c in range(CHUNKS):
        overs[c].wait()
        narrowed[c] = merged[c, bit] + next_in[c]
        for d in range(1, quarter):
            other = lax.rem(kk + d, quarter)
            number = c * (quarter - 1) + d - 1
            groups.append(remote(
                narrowed.at[c, other], group_in.at[number],
                group_send.at[number], group_recv.at[number],
                (4 * other + 2 * bit + parity, spec),
            ))
            groups[-1].start()

    @pl.loop(0, width_x)
    def _(x):
        low = cells_of(pl.multiple_of(x * width_y, 8), 8)
        high = cells_of(pl.multiple_of(x * width_y + width_y - 8, 8), 8)
        ylow_ref[x] = low[:halo * fields]
        yhigh_ref[x] = high[(8 - halo) * fields:]

    spreads = []
    for c in range(CHUNKS):
        total = narrowed[c, kk]
        for d in range(1, quarter):
            number = c * (quarter - 1) + d - 1
            groups[number].wait()
            total = total + group_in[number]
        feat_ref[spec, c] = total
        for d in range(1, specs):
            number = c * (specs - 1) + d - 1
            spreads.append(remote(
                feat_ref.at[spec, c], feat_ref.at[spec, c],
                spec_send.at[number], spec_recv.at[number],
                (col, lax.rem(spec + d, specs)),
            ))
            spreads[-1].start()
    rows = ylow_ref.shape[1]
    row_end = xlow_ref.shape[1]
    sides = [
        copy(xlow_ref, xh_ref, 1, (west, spec)),
        copy(xhigh_ref, xl_ref, 2, (east, spec)),
        copy(ylow_ref, yh_ref.at[pl.ds(halo, width_x)], 3, (col, south)),
        copy(yhigh_ref, yl_ref.at[pl.ds(halo, width_x)], 4, (col, north)),
    ]
    for one in sides:
        one.start()

    @pl.loop(0, width_x)
    def _(x):
        piece = air_ref[:, pl.ds(pl.multiple_of(x * width_y, 8), width_y), :]
        first[x + halo, halo:halo + width_y] = pltpu.einshape("fcl->cfl", piece)

    for c in range(CHUNKS):
        for d in range(1, specs):
            number = c * (specs - 1) + d - 1
            spreads[number].wait_send()
            source = lax.rem(spec + specs - d, specs)
            remote(
                feat_ref.at[source, c], feat_ref.at[source, c],
                spec_send.at[number], spec_recv.at[number],
                (col, lax.rem(spec + d, specs)),
            ).wait_recv()

    for s in range(specs):
        for c in range(CHUNKS):
            start = s * block + c * piece_rows
            feats[start:start + piece_rows, :] = feat_ref[s, c].astype(F32)
    slant = jnp.concatenate(
        [feats[s * block + inputs * share:(s + 1) * block, :] for s in range(specs)], axis=0
    )[:, :1]
    weight = jnp.concatenate(
        [in_weight_ref[...].astype(F32), jnp.zeros((1, in_weight_ref.shape[1]), F32)], axis=0
    ).astype(BF16)
    mid_weight = mid_weight_ref[...]
    in_bias, mid_bias = in_bias_ref[...], mid_bias_ref[...]

    for s in range(specs):
        @pl.loop(0, share // 8)
        def _(group):
            ones = []
            for j in range(8):
                column = feats[pl.ds(s * block + group * 8 + j, fields, stride=share), :]
                summed = lax.dot_general(
                    column.astype(BF16), weight, (((0,), (0,)), ((), ())),
                    preferred_element_type=F32,
                )
                ones.append(silu(summed + in_bias).astype(BF16))
            middle = jnp.dot(
                jnp.concatenate(ones, axis=0), mid_weight, preferred_element_type=F32
            )
            middle = silu(middle + mid_bias)
            for j in range(8):
                start = s * share + group * 8 + j
                hidden[pl.ds(start, levels, stride=columns), :] = (
                    middle[j * levels:(j + 1) * levels]
                )

    for one in sides:
        one.wait()
    corners = [
        copy(xl_ref.at[:, pl.ds(0, rows)], yh_ref.at[pl.ds(0, halo)], 5, (col, south)),
        copy(xh_ref.at[:, pl.ds(0, rows)], yh_ref.at[pl.ds(halo + width_x, halo)], 6, (col, south)),
        copy(xl_ref.at[:, pl.ds(row_end - rows, rows)], yl_ref.at[pl.ds(0, halo)], 7, (col, north)),
        copy(xh_ref.at[:, pl.ds(row_end - rows, rows)], yl_ref.at[pl.ds(halo + width_x, halo)], 8,
             (col, north)),
    ]
    for one in corners:
        one.start()
    fetch.wait()

    absorption = absorption_ref[...]
    down_rate = -LOG2_E * (absorption / slant)
    up_rate = -DIFFUSIVITY * LOG2_E * absorption
    out_bias = out_bias_ref[...]
    lane = lax.broadcasted_iota(jnp.int32, (columns, levels), 1)
    unroll = 16

    def downward(part, carry):
        now, kept = carry
        for j in range(unroll):
            level = part * unroll + j
            start = pl.multiple_of(level * columns, 8)
            two = hidden[pl.ds(start, columns), :].astype(BF16)
            logits = lax.dot_general(
                two, out_weight[level], (((1,), (1,)), ((), ())), preferred_element_type=F32
            ) + out_bias
            small = jnp.exp(-jnp.abs(logits))
            soft = jnp.maximum(logits, 0.0) + jnp.where(
                small < 1e-3, small - 0.5 * small * small, jnp.log(1.0 + small)
            )
            below = now * jnp.exp2(down_rate * soft)
            upward[level] = jnp.exp2(up_rate * soft)
            gone = jnp.sum(now - below, axis=1, keepdims=True)
            kept = jnp.where(lane == level, gone, kept)
            now = below
        return now, kept

    def upwards(part, carry):
        now, kept = carry
        for j in range(unroll):
            level = levels - 1 - (part * unroll + j)
            above = now * upward[level]
            gone = jnp.sum(now - above, axis=1, keepdims=True)
            kept = jnp.where(lane == level, kept + gone, kept)
            now = above
        return now, kept

    now, kept = lax.fori_loop(
        0, levels // unroll, downward,
        (flux_ref[...] * slant, jnp.zeros((columns, levels), F32)),
    )
    _, kept = lax.fori_loop(0, levels // unroll, upwards, (ALBEDO * now, kept))
    part_ref[...] = kept.reshape(specs, share, levels)

    backs = []
    for d in range(1, specs):
        other = lax.rem(spec + d, specs)
        backs.append(remote(
            part_ref.at[other], spec_in.at[d - 1], back_send.at[d - 1], back_recv.at[d - 1],
            (col, other),
        ))
    for one in backs:
        one.start()

    for one in corners:
        one.wait()

    def unpacked(value, count):
        return value.astype(F32).reshape(count, fields, levels)

    for x in range(halo):
        first[x, halo:halo + width_y] = unpacked(xl_ref[x], width_y)
        first[halo + width_x + x, halo:halo + width_y] = unpacked(xh_ref[x], width_y)

    @pl.loop(0, wide_x)
    def _(x):
        first[x, 0:halo] = unpacked(yl_ref[x], halo)
        first[x, halo + width_y:wide_y] = unpacked(yh_ref[x], halo)

    rate_x, rate_y = courant_x_ref[...], courant_y_ref[...]
    spread_x = 0.5 * rate_x * rate_x + DIFFUSION
    spread_y = 0.5 * rate_y * rate_y + DIFFUSION

    def wide(row):
        return jnp.broadcast_to(row, (fields, levels))[None]

    keep = wide(1.0 - 2.0 * spread_x - 2.0 * spread_y)
    from_east, from_west = wide(spread_x - 0.5 * rate_x), wide(spread_x + 0.5 * rate_x)
    from_north, from_south = wide(spread_y - 0.5 * rate_y), wide(spread_y + 0.5 * rate_y)
    buffers = (first, second)

    def advance(section):
        source, target = buffers[section % 2], buffers[(section + 1) % 2]
        low, high = section + 1, wide_y - section - 1
        last = section == SECTIONS - 1

        @pl.loop(section + 1, wide_x - section - 1)
        def _(x):
            value = (
                keep * source[x, low:high]
                + from_east * source[x + 1, low:high]
                + from_west * source[x - 1, low:high]
                + from_north * source[x, low + 1:high + 1]
                + from_south * source[x, low - 1:high - 1]
            )
            if last:
                state_ref[x - halo] = value
            else:
                target[x, low:high] = value

    for one in backs:
        one.wait()
    total = part_ref[spec]
    for d in range(1, specs):
        total = total + spec_in[d - 1]
    heat_ref[parity, k] = total
    gathers = []
    for d in range(1, half):
        gathers.append(remote(
            heat_ref.at[parity, k], heat_ref.at[parity, k], heat_send.at[d], heat_recv.at[d],
            (2 * lax.rem(k + d, half) + parity, spec),
        ))
    for one in gathers:
        one.start()
    for section in range(SECTIONS - 1):
        advance(section)
    for d in range(1, half):
        gathers[d - 1].wait_send()
        source = lax.rem(k + half - d, half)
        remote(
            heat_ref.at[parity, source], heat_ref.at[parity, source],
            heat_send.at[d], heat_recv.at[d],
            (2 * lax.rem(k + d, half) + parity, spec),
        ).wait_recv()
    last = remote(
        heat_ref.at[parity], heat_ref.at[parity], heat_send.at[0], heat_recv.at[0],
        (partner, spec),
    )
    last.start()
    advance(SECTIONS - 1)
    last.wait_send()
    remote(
        heat_ref.at[1 - parity], heat_ref.at[1 - parity], heat_send.at[0], heat_recv.at[0],
        (partner, spec),
    ).wait_recv()


def finish_kernel(share, width_y, state_in_ref, index_ref, count_ref, heat_ref,
                  state_ref, grid_ref):
    cells, levels = grid_ref.shape
    width_x = cells // width_y
    col, spec = lax.axis_index("cols"), lax.axis_index("spec")
    half = heat_ref.shape[1]
    before = pl.program_id(0) * cells
    grid = jnp.zeros((cells, levels), F32)
    for parity in range(2):
        ranks = rank_column([2 * k + parity for k in range(half)], share)
        cell = cell_column(ranks, count_ref[...], index_ref[0], spec, col)
        slots = cell.shape[0]
        lane = (lax.broadcasted_iota(jnp.int32, (slots, cells), 1) + before).astype(F32)
        choose = jnp.where(cell == lane, 1.0, 0.0).astype(BF16)
        rows = heat_ref[parity].reshape(slots, levels)
        upper = rows.astype(BF16)
        lower = (rows - upper.astype(F32)).astype(BF16)
        for piece in (upper, lower):
            grid = grid + lax.dot_general(
                choose, piece, (((0,), (0,)), ((), ())), preferred_element_type=F32
            )
    grid_ref[...] = grid
    for x in range(width_x):
        start = x * width_y
        block = pltpu.einshape("cfl->fcl", state_in_ref[x])
        state_ref[:, start:start + width_y, :] = block
        state_ref[0, start:start + width_y, :] = block[0] + grid[start:start + width_y]


def on_device(
    air_state,
    courant_x,
    courant_y,
    cos_zenith,
    sun_index,
    sun_count,
    in_weight,
    in_bias,
    mid_weight,
    mid_bias,
    out_weight,
    out_bias,
    absorption,
    solar_flux,
):
    fields, width_x, width_y, levels = air_state.shape
    cells = width_x * width_y
    cols, specs = lax.axis_size("cols"), lax.axis_size("spec")
    half, quarter = cols // 2, cols // 4
    share = sun_index.shape[2] // 4
    halo = SECTIONS
    block = fields * share
    piece = block // CHUNKS
    columns = specs * share
    points, hidden_size = out_weight.shape[1], out_weight.shape[2]
    air = air_state.reshape(fields, cells, levels)
    vmem = pl.BlockSpec(memory_space=pltpu.VMEM)
    dma = pltpu.SemaphoreType.DMA
    x_halo = pltpu.VMEM((halo, width_y * fields, levels), BF16)
    y_edge = pltpu.VMEM((width_x, halo * fields, levels), BF16)
    y_halo = pltpu.VMEM((width_x + 2 * halo, halo * fields, levels), BF16)
    wide = pltpu.VMEM((width_x + 2 * halo, width_y + 2 * halo, fields, levels), F32)

    state, heats = pl.pallas_call(
        functools.partial(main_kernel, cols, specs, share, halo, width_y),
        out_shape=(
            jax.ShapeDtypeStruct((width_x, width_y, fields, levels), F32),
            jax.ShapeDtypeStruct((2, half, share, levels), F32),
        ),
        in_specs=[vmem] * 10 + [pl.BlockSpec(memory_space=pl.ANY)] + [vmem] * 3,
        out_specs=(vmem, vmem),
        scratch_shapes=[
            pltpu.VMEM((CHUNKS, 2, quarter, piece, levels), BF16),
            x_halo,
            x_halo,
            y_edge,
            y_edge,
            pltpu.VMEM((fields // CHUNKS, half * share, levels), F32),
            pltpu.VMEM((specs, CHUNKS, piece, levels), BF16),
            x_halo,
            x_halo,
            y_halo,
            y_halo,
            pltpu.VMEM((CHUNKS, 2, quarter, piece, levels), BF16),
            pltpu.VMEM((CHUNKS, 2, quarter, piece, levels), BF16),
            pltpu.VMEM((CHUNKS, quarter, piece, levels), BF16),
            pltpu.VMEM((CHUNKS, quarter, piece, levels), BF16),
            pltpu.VMEM((CHUNKS * (quarter - 1), piece, levels), BF16),
            pltpu.VMEM(out_weight.shape, BF16),
            pltpu.VMEM((specs * block, levels), F32),
            pltpu.VMEM((levels * columns, hidden_size), F32),
            pltpu.VMEM((levels, columns, points), F32),
            pltpu.VMEM((specs, share, levels), F32),
            pltpu.VMEM((specs - 1, share, levels), F32),
            wide,
            wide,
            dma,
            dma((10 + 2 * CHUNKS,)),
            dma((10 + 2 * CHUNKS,)),
            dma((CHUNKS * (quarter - 1),)),
            dma((CHUNKS * (quarter - 1),)),
            dma((CHUNKS * (specs - 1),)),
            dma((CHUNKS * (specs - 1),)),
            dma((specs - 1,)),
            dma((specs - 1,)),
            dma((half,)),
            dma((half,)),
        ],
        compiler_params=pltpu.CompilerParams(
            vmem_limit_bytes=VMEM_LIMIT, collective_id=0, has_side_effects=True
        ),
        name="main",
    )(air, cos_zenith, sun_index, sun_count, courant_x.reshape(1, -1), courant_y.reshape(1, -1),
      in_weight, in_bias.reshape(1, -1), mid_weight, mid_bias.reshape(1, -1), out_weight,
      out_bias.reshape(1, -1), absorption.reshape(1, -1), solar_flux.reshape(1, -1))

    steps = 4
    state, grid = pl.pallas_call(
        functools.partial(finish_kernel, share, width_y),
        out_shape=(
            jax.ShapeDtypeStruct((fields, cells, levels), F32),
            jax.ShapeDtypeStruct((cells, levels), F32),
        ),
        grid=(steps,),
        in_specs=[
            pl.BlockSpec((width_x // steps, width_y, fields, levels), lambda i: (i, 0, 0, 0)),
            pl.BlockSpec(sun_index.shape, lambda i: (0, 0, 0)),
            pl.BlockSpec(sun_count.shape, lambda i: (0, 0)),
            pl.BlockSpec(heats.shape, lambda i: (0, 0, 0, 0)),
        ],
        out_specs=(
            pl.BlockSpec((fields, cells // steps, levels), lambda i: (0, i, 0)),
            pl.BlockSpec((cells // steps, levels), lambda i: (i, 0)),
        ),
        compiler_params=pltpu.CompilerParams(vmem_limit_bytes=VMEM_LIMIT),
        name="finish",
    )(state, sun_index, sun_count, heats)
    return (
        state.reshape(air_state.shape),
        grid.reshape(width_x, width_y, levels),
    )


def solution(mesh):
    placed = (
        P(None, "cols", "spec", None),
        P(),
        P(),
        P("cols", "spec"),
        P("cols", "spec", None),
        P(),
        P(),
        P(),
        P(),
        P(),
        P(None, "spec", None),
        P("spec"),
        P("spec"),
        P("spec"),
    )
    return jax.shard_map(
        on_device,
        mesh=mesh,
        in_specs=placed,
        out_specs=(P(None, "cols", "spec", None), P("cols", "spec", None)),
        check_vma=False,
    )
```

```python
import functools

import jax
import jax.numpy as jnp
from jax import lax
from jax.experimental import pallas as pl
from jax.experimental.pallas import tpu as pltpu
from jax.sharding import PartitionSpec as P

SECTIONS = 4
CHUNKS = 2
LOG2_E = 1.4426950408889634
DIFFUSION = 0.05
ALBEDO = 0.3
DIFFUSIVITY = 1.66
MESH = pl.DeviceIdType.MESH
F32 = jnp.float32
BF16 = jnp.bfloat16
VMEM_LIMIT = 56 * 1024 * 1024


def cell_column(ranks, counts, index_row, spec, col):
    row = lax.broadcasted_iota(jnp.int32, counts.shape, 0)
    column = lax.broadcasted_iota(jnp.int32, counts.shape, 1)
    values = jnp.where(row == spec, counts, 0).astype(F32)
    offset = jnp.sum(jnp.where(column < col, values, 0.0), axis=(0, 1), keepdims=True)
    own = jnp.sum(jnp.where(column == col, values, 0.0), axis=(0, 1), keepdims=True)
    place = lax.broadcasted_iota(jnp.int32, (1, index_row.shape[1]), 1).astype(F32)
    table = jnp.where(place < own, index_row.astype(F32) + 1.0, 0.0)
    found = jnp.where(ranks - offset == place, table, 0.0)
    return jnp.sum(found, axis=1, keepdims=True) - 1.0


def rank_column(firsts, share):
    within = lax.broadcasted_iota(jnp.int32, (share, 1), 0)
    return jnp.concatenate([(first * share + within).astype(F32) for first in firsts], axis=0)


def silu(value):
    half = 0.5 * value
    return half + half * jnp.tanh(half)


def remote(src, dst, send, recv, peer):
    return pltpu.make_async_remote_copy(
        src_ref=src, dst_ref=dst, send_sem=send, recv_sem=recv, device_id=peer, device_id_type=MESH
    )


def main_kernel(cols, specs, share, halo, width_y,
                air_ref, cos_ref, index_ref, count_ref, courant_x_ref, courant_y_ref,
                in_weight_ref, in_bias_ref, mid_weight_ref, mid_bias_ref, out_weight_ref,
                out_bias_ref, absorption_ref, flux_ref,
                state_ref, heat_ref,
                send_ref, xlow_ref, xhigh_ref, ylow_ref, yhigh_ref, picked,
                feat_ref, xl_ref, xh_ref, yl_ref, yh_ref,
                pair_in, merged, next_in, narrowed, group_in,
                out_weight, feats, hidden, upward, part_ref, spec_in, first, second,
                weight_sem, send_sem, recv_sem, group_send, group_recv, spec_send, spec_recv,
                back_send, back_recv, heat_send, heat_recv):
    fields, cells, levels = air_ref.shape
    width_x = cells // width_y
    inputs = fields - 1
    wide_x, wide_y = width_x + 2 * halo, width_y + 2 * halo
    columns = specs * share
    block = fields * share
    group_fields = fields // CHUNKS
    piece_rows = group_fields * share
    col, spec = lax.axis_index("cols"), lax.axis_index("spec")
    half, quarter = cols // 2, cols // 4
    parity, k = lax.rem(col, 2), lax.div(col, 2)
    bit, kk = lax.rem(k, 2), lax.div(k, 2)
    partner = col + 1 - 2 * parity
    across = col + 2 - 4 * bit
    east, west = lax.rem(col + 1, cols), lax.rem(col + cols - 1, cols)
    north, south = lax.rem(spec + 1, specs), lax.rem(spec + specs - 1, specs)
    barrier = pltpu.get_barrier_semaphore()
    peers = [(partner, spec), (east, spec), (west, spec)]
    peers += [(2 * lax.rem(k + d, half) + parity, spec) for d in range(1, half)]
    peers += [(col, lax.rem(spec + d, specs)) for d in range(1, specs)]
    for peer in peers:
        pl.semaphore_signal(barrier, inc=1, device_id=peer, device_id_type=MESH)
    fetch = pltpu.make_async_copy(out_weight_ref, out_weight, weight_sem)
    fetch.start()

    def copy(src, dst, number, peer):
        return remote(src, dst, send_sem.at[number], recv_sem.at[number], peer)

    counts, index_row = count_ref[...], index_ref[0]

    def choice(which):
        ranks = rank_column(
            [4 * c + 2 * b + which for b in range(2) for c in range(quarter)], share
        )
        cell = cell_column(ranks, counts, index_row, spec, col)
        slots = cell.shape[0]
        lane = lax.broadcasted_iota(jnp.int32, (slots, cells), 1).astype(F32)
        choose = jnp.where(cell == lane, 1.0, 0.0).astype(BF16)
        return cell, choose

    def pack(chosen, chunk):
        cell, choose = chosen
        slots = cell.shape[0]
        for at in range(group_fields):
            i = chunk * group_fields + at
            if i < inputs:
                picked[at] = jnp.dot(
                    choose, air_ref[i].astype(BF16), preferred_element_type=F32
                )
                continue
            cell_x = jnp.floor((cell + 0.5) * (1.0 / width_y))
            cell_y = cell - cell_x * width_y
            lane_x = lax.broadcasted_iota(jnp.int32, (slots, width_x), 1).astype(F32)
            lane_y = lax.broadcasted_iota(jnp.int32, (slots, width_y), 1).astype(F32)
            by_x = jnp.dot(
                jnp.where(cell_x == lane_x, 1.0, 0.0).astype(BF16),
                cos_ref[...].astype(BF16),
                preferred_element_type=F32,
            )
            slant = jnp.sum(jnp.where(cell_y == lane_y, by_x, 0.0), axis=1, keepdims=True)
            picked[at] = jnp.broadcast_to(slant, (slots, levels))
        blocks = []
        for at in range(half):
            piece = picked[:, at * share:(at + 1) * share, :]
            blocks.append(piece.reshape(piece_rows, levels).astype(BF16)[None])
        return jnp.concatenate(blocks, axis=0).reshape(2, quarter, piece_rows, levels)

    chosen = choice(1 - parity)
    pairs = [
        copy(send_ref.at[c], pair_in.at[c], 10 + c, (partner, spec)) for c in range(CHUNKS)
    ]
    overs = [
        copy(merged.at[c, 1 - bit], next_in.at[c], 10 + CHUNKS + c, (across, spec))
        for c in range(CHUNKS)
    ]
    for c in range(CHUNKS):
        send_ref[c] = pack(chosen, c)
        if c == 0:
            pl.semaphore_wait(barrier, len(peers))
        pairs[c].start()
    chosen = choice(parity)
    for c in range(CHUNKS):
        merged[c] = pack(chosen, c)
        pairs[c].wait()
        merged[c] = merged[c] + pair_in[c]
        overs[c].start()

    def cells_of(start, count):
        piece = air_ref[:, pl.ds(start, count), :]
        return pltpu.einshape("fcl->cfl", piece).reshape(count * fields, levels).astype(BF16)

    for x in range(halo):
        xlow_ref[x] = cells_of(x * width_y, width_y)
        xhigh_ref[x] = cells_of((width_x - halo + x) * width_y, width_y)
    groups = []
    for c in range(CHUNKS):
        overs[c].wait()
        narrowed[c] = merged[c, bit] + next_in[c]
        for d in range(1, quarter):
            other = lax.rem(kk + d, quarter)
            number = c * (quarter - 1) + d - 1
            groups.append(remote(
                narrowed.at[c, other], group_in.at[number],
                group_send.at[number], group_recv.at[number],
                (4 * other + 2 * bit + parity, spec),
            ))
            groups[-1].start()

    @pl.loop(0, width_x)
    def _(x):
        low = cells_of(pl.multiple_of(x * width_y, 8), 8)
        high = cells_of(pl.multiple_of(x * width_y + width_y - 8, 8), 8)
        ylow_ref[x] = low[:halo * fields]
        yhigh_ref[x] = high[(8 - halo) * fields:]

    spreads = []
    for c in range(CHUNKS):
        total = narrowed[c, kk]
        for d in range(1, quarter):
            number = c * (quarter - 1) + d - 1
            groups[number].wait()
            total = total + group_in[number]
        feat_ref[spec, c] = total
        for d in range(1, specs):
            number = c * (specs - 1) + d - 1
            spreads.append(remote(
                feat_ref.at[spec, c], feat_ref.at[spec, c],
                spec_send.at[number], spec_recv.at[number],
                (col, lax.rem(spec + d, specs)),
            ))
            spreads[-1].start()
    rows = ylow_ref.shape[1]
    row_end = xlow_ref.shape[1]
    sides = [
        copy(xlow_ref, xh_ref, 1, (west, spec)),
        copy(xhigh_ref, xl_ref, 2, (east, spec)),
        copy(ylow_ref, yh_ref.at[pl.ds(halo, width_x)], 3, (col, south)),
        copy(yhigh_ref, yl_ref.at[pl.ds(halo, width_x)], 4, (col, north)),
    ]
    for one in sides:
        one.start()

    @pl.loop(0, width_x)
    def _(x):
        piece = air_ref[:, pl.ds(pl.multiple_of(x * width_y, 8), width_y), :]
        first[x + halo, halo:halo + width_y] = pltpu.einshape("fcl->cfl", piece)

    for c in range(CHUNKS):
        for d in range(1, specs):
            number = c * (specs - 1) + d - 1
            spreads[number].wait_send()
            source = lax.rem(spec + specs - d, specs)
            remote(
                feat_ref.at[source, c], feat_ref.at[source, c],
                spec_send.at[number], spec_recv.at[number],
                (col, lax.rem(spec + d, specs)),
            ).wait_recv()

    for s in range(specs):
        for c in range(CHUNKS):
            start = s * block + c * piece_rows
            feats[start:start + piece_rows, :] = feat_ref[s, c].astype(F32)
    slant = jnp.concatenate(
        [feats[s * block + inputs * share:(s + 1) * block, :] for s in range(specs)], axis=0
    )[:, :1]
    weight = jnp.concatenate(
        [in_weight_ref[...].astype(F32), jnp.zeros((1, in_weight_ref.shape[1]), F32)], axis=0
    ).astype(BF16)
    mid_weight = mid_weight_ref[...]
    in_bias, mid_bias = in_bias_ref[...], mid_bias_ref[...]

    for s in range(specs):
        @pl.loop(0, share // 8)
        def _(group):
            ones = []
            for j in range(8):
                column = feats[pl.ds(s * block + group * 8 + j, fields, stride=share), :]
                summed = lax.dot_general(
                    column.astype(BF16), weight, (((0,), (0,)), ((), ())),
                    preferred_element_type=F32,
                )
                ones.append(silu(summed + in_bias).astype(BF16))
            middle = jnp.dot(
                jnp.concatenate(ones, axis=0), mid_weight, preferred_element_type=F32
            )
            middle = silu(middle + mid_bias)
            for j in range(8):
                start = s * share + group * 8 + j
                hidden[pl.ds(start, levels, stride=columns), :] = (
                    middle[j * levels:(j + 1) * levels]
                )

    for one in sides:
        one.wait()
    corners = [
        copy(xl_ref.at[:, pl.ds(0, rows)], yh_ref.at[pl.ds(0, halo)], 5, (col, south)),
        copy(xh_ref.at[:, pl.ds(0, rows)], yh_ref.at[pl.ds(halo + width_x, halo)], 6, (col, south)),
        copy(xl_ref.at[:, pl.ds(row_end - rows, rows)], yl_ref.at[pl.ds(0, halo)], 7, (col, north)),
        copy(xh_ref.at[:, pl.ds(row_end - rows, rows)], yl_ref.at[pl.ds(halo + width_x, halo)], 8,
             (col, north)),
    ]
    for one in corners:
        one.start()
    fetch.wait()

    absorption = absorption_ref[...]
    down_rate = -LOG2_E * (absorption / slant)
    up_rate = -DIFFUSIVITY * LOG2_E * absorption
    out_bias = out_bias_ref[...]
    lane = lax.broadcasted_iota(jnp.int32, (columns, levels), 1)
    unroll = 16

    def downward(part, carry):
        now, kept = carry
        for j in range(unroll):
            level = part * unroll + j
            start = pl.multiple_of(level * columns, 8)
            two = hidden[pl.ds(start, columns), :].astype(BF16)
            logits = lax.dot_general(
                two, out_weight[level], (((1,), (1,)), ((), ())), preferred_element_type=F32
            ) + out_bias
            small = jnp.exp(-jnp.abs(logits))
            soft = jnp.maximum(logits, 0.0) + jnp.where(
                small < 1e-3, small - 0.5 * small * small, jnp.log(1.0 + small)
            )
            below = now * jnp.exp2(down_rate * soft)
            upward[level] = jnp.exp2(up_rate * soft)
            gone = jnp.sum(now - below, axis=1, keepdims=True)
            kept = jnp.where(lane == level, gone, kept)
            now = below
        return now, kept

    def upwards(part, carry):
        now, kept = carry
        for j in range(unroll):
            level = levels - 1 - (part * unroll + j)
            above = now * upward[level]
            gone = jnp.sum(now - above, axis=1, keepdims=True)
            kept = jnp.where(lane == level, kept + gone, kept)
            now = above
        return now, kept

    now, kept = lax.fori_loop(
        0, levels // unroll, downward,
        (flux_ref[...] * slant, jnp.zeros((columns, levels), F32)),
    )
    _, kept = lax.fori_loop(0, levels // unroll, upwards, (ALBEDO * now, kept))
    part_ref[...] = kept.reshape(specs, share, levels)

    backs = []
    for d in range(1, specs):
        other = lax.rem(spec + d, specs)
        backs.append(remote(
            part_ref.at[other], spec_in.at[d - 1], back_send.at[d - 1], back_recv.at[d - 1],
            (col, other),
        ))
    for one in backs:
        one.start()

    for one in corners:
        one.wait()

    def unpacked(value, count):
        return value.astype(F32).reshape(count, fields, levels)

    for x in range(halo):
        first[x, halo:halo + width_y] = unpacked(xl_ref[x], width_y)
        first[halo + width_x + x, halo:halo + width_y] = unpacked(xh_ref[x], width_y)

    @pl.loop(0, wide_x)
    def _(x):
        first[x, 0:halo] = unpacked(yl_ref[x], halo)
        first[x, halo + width_y:wide_y] = unpacked(yh_ref[x], halo)

    rate_x, rate_y = courant_x_ref[...], courant_y_ref[...]
    spread_x = 0.5 * rate_x * rate_x + DIFFUSION
    spread_y = 0.5 * rate_y * rate_y + DIFFUSION

    def wide(row):
        return jnp.broadcast_to(row, (fields, levels))[None]

    keep = wide(1.0 - 2.0 * spread_x - 2.0 * spread_y)
    from_east, from_west = wide(spread_x - 0.5 * rate_x), wide(spread_x + 0.5 * rate_x)
    from_north, from_south = wide(spread_y - 0.5 * rate_y), wide(spread_y + 0.5 * rate_y)
    buffers = (first, second)

    def advance(section):
        source, target = buffers[section % 2], buffers[(section + 1) % 2]
        low, high = section + 1, wide_y - section - 1
        last = section == SECTIONS - 1

        @pl.loop(section + 1, wide_x - section - 1)
        def _(x):
            value = (
                keep * source[x, low:high]
                + from_east * source[x + 1, low:high]
                + from_west * source[x - 1, low:high]
                + from_north * source[x, low + 1:high + 1]
                + from_south * source[x, low - 1:high - 1]
            )
            if last:
                state_ref[x - halo] = value
            else:
                target[x, low:high] = value

    for one in backs:
        one.wait()
    total = part_ref[spec]
    for d in range(1, specs):
        total = total + spec_in[d - 1]
    heat_ref[parity, k] = total
    gathers = []
    for d in range(1, half):
        gathers.append(remote(
            heat_ref.at[parity, k], heat_ref.at[parity, k], heat_send.at[d], heat_recv.at[d],
            (2 * lax.rem(k + d, half) + parity, spec),
        ))
    for one in gathers:
        one.start()
    for section in range(SECTIONS - 1):
        advance(section)
    for d in range(1, half):
        gathers[d - 1].wait_send()
        source = lax.rem(k + half - d, half)
        remote(
            heat_ref.at[parity, source], heat_ref.at[parity, source],
            heat_send.at[d], heat_recv.at[d],
            (2 * lax.rem(k + d, half) + parity, spec),
        ).wait_recv()
    last = remote(
        heat_ref.at[parity], heat_ref.at[parity], heat_send.at[0], heat_recv.at[0],
        (partner, spec),
    )
    last.start()
    advance(SECTIONS - 1)
    last.wait_send()
    remote(
        heat_ref.at[1 - parity], heat_ref.at[1 - parity], heat_send.at[0], heat_recv.at[0],
        (partner, spec),
    ).wait_recv()


def finish_kernel(share, width_y, state_in_ref, index_ref, count_ref, heat_ref,
                  state_ref, grid_ref, whole_ref):
    rows, levels = grid_ref.shape
    cells = whole_ref.shape[0]
    width_x = rows // width_y
    step = pl.program_id(0)

    @pl.when(step == 0)
    def _():
        col, spec = lax.axis_index("cols"), lax.axis_index("spec")
        half = heat_ref.shape[1]
        ranks = rank_column([2 * k + parity for parity in range(2) for k in range(half)], share)
        cell = cell_column(ranks, count_ref[...], index_ref[0], spec, col)
        slots = cell.shape[0]
        across = jnp.transpose(jnp.broadcast_to(cell, (slots, 128)))[:1]
        owner = lax.broadcasted_iota(jnp.int32, (cells, slots), 0).astype(F32)
        choose = jnp.where(across == owner, 1.0, 0.0).astype(BF16)
        heats = heat_ref[...].reshape(slots, levels)
        upper = heats.astype(BF16)
        lower = (heats - upper.astype(F32)).astype(BF16)
        whole_ref[...] = jnp.dot(choose, upper, preferred_element_type=F32) + jnp.dot(
            choose, lower, preferred_element_type=F32
        )

    grid_ref[...] = whole_ref[pl.ds(pl.multiple_of(step * rows, 8), rows), :]
    for x in range(width_x):
        start = x * width_y
        block = pltpu.einshape("cfl->fcl", state_in_ref[x])
        state_ref[:, start:start + width_y, :] = block
        state_ref[0, start:start + width_y, :] = block[0] + grid_ref[start:start + width_y, :]


def on_device(
    air_state,
    courant_x,
    courant_y,
    cos_zenith,
    sun_index,
    sun_count,
    in_weight,
    in_bias,
    mid_weight,
    mid_bias,
    out_weight,
    out_bias,
    absorption,
    solar_flux,
):
    fields, width_x, width_y, levels = air_state.shape
    cells = width_x * width_y
    cols, specs = lax.axis_size("cols"), lax.axis_size("spec")
    half, quarter = cols // 2, cols // 4
    share = sun_index.shape[2] // 4
    halo = SECTIONS
    block = fields * share
    piece = block // CHUNKS
    columns = specs * share
    points, hidden_size = out_weight.shape[1], out_weight.shape[2]
    air = air_state.reshape(fields, cells, levels)
    vmem = pl.BlockSpec(memory_space=pltpu.VMEM)
    dma = pltpu.SemaphoreType.DMA
    x_halo = pltpu.VMEM((halo, width_y * fields, levels), BF16)
    y_edge = pltpu.VMEM((width_x, halo * fields, levels), BF16)
    y_halo = pltpu.VMEM((width_x + 2 * halo, halo * fields, levels), BF16)
    wide = pltpu.VMEM((width_x + 2 * halo, width_y + 2 * halo, fields, levels), F32)

    state, heats = pl.pallas_call(
        functools.partial(main_kernel, cols, specs, share, halo, width_y),
        out_shape=(
            jax.ShapeDtypeStruct((width_x, width_y, fields, levels), F32),
            jax.ShapeDtypeStruct((2, half, share, levels), F32),
        ),
        in_specs=[vmem] * 10 + [pl.BlockSpec(memory_space=pl.ANY)] + [vmem] * 3,
        out_specs=(vmem, vmem),
        scratch_shapes=[
            pltpu.VMEM((CHUNKS, 2, quarter, piece, levels), BF16),
            x_halo,
            x_halo,
            y_edge,
            y_edge,
            pltpu.VMEM((fields // CHUNKS, half * share, levels), F32),
            pltpu.VMEM((specs, CHUNKS, piece, levels), BF16),
            x_halo,
            x_halo,
            y_halo,
            y_halo,
            pltpu.VMEM((CHUNKS, 2, quarter, piece, levels), BF16),
            pltpu.VMEM((CHUNKS, 2, quarter, piece, levels), BF16),
            pltpu.VMEM((CHUNKS, quarter, piece, levels), BF16),
            pltpu.VMEM((CHUNKS, quarter, piece, levels), BF16),
            pltpu.VMEM((CHUNKS * (quarter - 1), piece, levels), BF16),
            pltpu.VMEM(out_weight.shape, BF16),
            pltpu.VMEM((specs * block, levels), F32),
            pltpu.VMEM((levels * columns, hidden_size), F32),
            pltpu.VMEM((levels, columns, points), F32),
            pltpu.VMEM((specs, share, levels), F32),
            pltpu.VMEM((specs - 1, share, levels), F32),
            wide,
            wide,
            dma,
            dma((10 + 2 * CHUNKS,)),
            dma((10 + 2 * CHUNKS,)),
            dma((CHUNKS * (quarter - 1),)),
            dma((CHUNKS * (quarter - 1),)),
            dma((CHUNKS * (specs - 1),)),
            dma((CHUNKS * (specs - 1),)),
            dma((specs - 1,)),
            dma((specs - 1,)),
            dma((half,)),
            dma((half,)),
        ],
        compiler_params=pltpu.CompilerParams(
            vmem_limit_bytes=VMEM_LIMIT, collective_id=0, has_side_effects=True
        ),
        name="main",
    )(air, cos_zenith, sun_index, sun_count, courant_x.reshape(1, -1), courant_y.reshape(1, -1),
      in_weight, in_bias.reshape(1, -1), mid_weight, mid_bias.reshape(1, -1), out_weight,
      out_bias.reshape(1, -1), absorption.reshape(1, -1), solar_flux.reshape(1, -1))

    steps = 4
    state, grid = pl.pallas_call(
        functools.partial(finish_kernel, share, width_y),
        out_shape=(
            jax.ShapeDtypeStruct((fields, cells, levels), F32),
            jax.ShapeDtypeStruct((cells, levels), F32),
        ),
        grid=(steps,),
        in_specs=[
            pl.BlockSpec((width_x // steps, width_y, fields, levels), lambda i: (i, 0, 0, 0)),
            pl.BlockSpec(sun_index.shape, lambda i: (0, 0, 0)),
            pl.BlockSpec(sun_count.shape, lambda i: (0, 0)),
            pl.BlockSpec(heats.shape, lambda i: (0, 0, 0, 0)),
        ],
        out_specs=(
            pl.BlockSpec((fields, cells // steps, levels), lambda i: (0, i, 0)),
            pl.BlockSpec((cells // steps, levels), lambda i: (i, 0)),
        ),
        scratch_shapes=[pltpu.VMEM((cells, levels), F32)],
        compiler_params=pltpu.CompilerParams(vmem_limit_bytes=VMEM_LIMIT),
        name="finish",
    )(state, sun_index, sun_count, heats)
    return (
        state.reshape(air_state.shape),
        grid.reshape(width_x, width_y, levels),
    )


def solution(mesh):
    placed = (
        P(None, "cols", "spec", None),
        P(),
        P(),
        P("cols", "spec"),
        P("cols", "spec", None),
        P(),
        P(),
        P(),
        P(),
        P(),
        P(None, "spec", None),
        P("spec"),
        P("spec"),
        P("spec"),
    )
    return jax.shard_map(
        on_device,
        mesh=mesh,
        in_specs=placed,
        out_specs=(P(None, "cols", "spec", None), P("cols", "spec", None)),
        check_vma=False,
    )
```
